512 devices in a mesh: gx: 4 (over z_lo), gy: 8 (over z_hi, core), zt: 16 (over x, y).
Axes of the slice: x: 4, y: 4, z: 16 (z_hi: 4, z_lo: 4; z = z_hi * 4 + z_lo), core: 2. Of those that a mesh axis runs over, the one named last changes fastest.
Arguments:
- near_null: bfloat16 [16, 32, 64, 2, 1152], P('gx', 'gy', 'zt'), may hold values from -6 to 6
- gauge: bfloat16 [16, 32, 64, 2, 144], P('gx', 'gy', 'zt'), may hold values from -6 to 6
- site_map: int32 [16, 32], P('zt'), may hold values from 0 to 31, each once within a row
Outputs:
- coarse_links: float32 [16, 32, 2, 9216], P('zt')
The draws below stay inside these ranges and needn't reach their ends.
Inputs may be any that keep to these rules, and one draw needn't show every extreme that they name: Each row of site_map names every coarse site 0 to 31 once.
All inputs are finite; a program needn't handle non-finite values.
Results may differ from the reference program's by a relative error of at most 0.0004.
Values may be sent and summed in bfloat16 or wider, within the bound.
No kernel may reach another device: no remote copies, remote signals or barrier semaphores. Data moves between devices by JAX's collectives and lax.ppermute only.
A program may use at most 64 MiB of HBM per device.

```python
import jax
import jax.numpy as jnp
import numpy as np
from jax import lax

AGG = 4
NVEC = 24
NT = 4
NX = 16
NY = 32
NZ = 64
NCOL = 32
N_ZT = 16


def shard_levels(key, dims, split, low, largest):
    gain = 1.0
    for dim, blocks in split:
        heights = jax.random.uniform(jax.random.fold_in(jax.random.fold_in(key, 6), dim), (blocks,), jnp.float32, low / len(split), largest / len(split))
        gain = gain * jnp.repeat(jnp.exp(heights), dims[dim] // blocks).reshape((-1,) + (1,) * (len(dims) - 1 - dim))
    return gain


def centred(rng, shape, deviation, reach, cuts=(), kind=jnp.bfloat16):
    loudness = shard_levels(rng, shape, cuts, -0.22, 0.18) if cuts else 1.0
    values = jax.random.normal(rng, shape, jnp.float32) * deviation * loudness
    return jnp.minimum(jnp.maximum(values, -reach), reach).astype(kind)


def setup_inputs(seed: int = 0) -> dict:
    arg_keys = jax.random.split(jax.random.key(seed), 4)
    return {
        "near_null": centred(arg_keys[0], (NX, NY, NZ, 2, NT * 12 * NVEC), 1.0, 6.0, ((0, 4), (1, 8), (2, 16))),
        "gauge": centred(arg_keys[1], (NX, NY, NZ, 2, 4 * NT * 9), 0.4, 6.0, ((0, 4), (1, 8), (2, 16))),
        "site_map": jax.vmap(lambda own: jax.random.permutation(own, NCOL))(jax.random.split(arg_keys[2], N_ZT)).reshape((N_ZT, NCOL)).astype(jnp.int32),
    }


def spin_blocks():
    nought = np.zeros((2, 2))
    return [(nought, np.array([[0.0, -1.0], [-1.0, 0.0]])), (np.array([[0.0, -1.0], [1.0, 0.0]]), nought), (nought, np.array([[-1.0, 0.0], [0.0, 1.0]])), (np.eye(2), nought)]

def chiral_layout(block):
    extent = block.shape[0]
    count = block.shape[-1] // (extent * 12)
    shaped = block.reshape(extent, extent, extent, 2, extent, 2, 2, 3, count)
    return jnp.transpose(shaped, (5, 3, 8, 7, 6, 0, 1, 2, 4))

def gauge_layout(block):
    extent = block.shape[0]
    shaped = block.reshape(extent, extent, extent, 2, 4, extent, 3, 3)
    return jnp.transpose(shaped, (4, 3, 6, 7, 0, 1, 2, 5)).astype(jnp.float32)

def gram_of(flat):
    flat_re = flat[:, 0]
    flat_im = flat[:, 1]
    gram_re = jnp.einsum('nkr,nlr->nkl', flat_re, flat_re, preferred_element_type=jnp.float32) + jnp.einsum('nkr,nlr->nkl', flat_im, flat_im, preferred_element_type=jnp.float32)
    gram_im = jnp.einsum('nkr,nlr->nkl', flat_re, flat_im, preferred_element_type=jnp.float32) - jnp.einsum('nkr,nlr->nkl', flat_im, flat_re, preferred_element_type=jnp.float32)
    return jnp.stack([gram_re, gram_im], axis=1)

def coefficients(gram_matrix, target):
    highest = lax.Precision.HIGHEST
    vector_count = gram_matrix.shape[-1]
    identity = jnp.eye(vector_count, dtype=gram_matrix.dtype)
    gram_re = gram_matrix[:, 0]
    gram_im = gram_matrix[:, 1]

    def gram_step(column, mixing):
        picked = lax.dynamic_index_in_dim(gram_matrix, column, 3, keepdims=False)
        unit_column = lax.dynamic_index_in_dim(identity, column, 1, keepdims=False)
        mixing_re = mixing[:, 0]
        mixing_im = mixing[:, 1]
        picked_re = picked[:, 0]
        picked_im = picked[:, 1]
        project_re = jnp.einsum('nlk,nl->nk', mixing_re, picked_re, precision=highest) + jnp.einsum('nlk,nl->nk', mixing_im, picked_im, precision=highest)
        project_im = jnp.einsum('nlk,nl->nk', mixing_re, picked_im, precision=highest) - jnp.einsum('nlk,nl->nk', mixing_im, picked_re, precision=highest)
        remain_re = unit_column - (jnp.einsum('nlk,nk->nl', mixing_re, project_re, precision=highest) - jnp.einsum('nlk,nk->nl', mixing_im, project_im, precision=highest))
        remain_im = -(jnp.einsum('nlk,nk->nl', mixing_re, project_im, precision=highest) + jnp.einsum('nlk,nk->nl', mixing_im, project_re, precision=highest))
        image_re = jnp.einsum('nlk,nk->nl', gram_re, remain_re, precision=highest) - jnp.einsum('nlk,nk->nl', gram_im, remain_im, precision=highest)
        image_im = jnp.einsum('nlk,nk->nl', gram_re, remain_im, precision=highest) + jnp.einsum('nlk,nk->nl', gram_im, remain_re, precision=highest)
        weight = lax.optimization_barrier(jnp.sum(remain_re * image_re + remain_im * image_im, axis=-1))
        factor = jnp.sqrt(target / weight)
        new_column = jnp.stack([remain_re, remain_im], axis=1) * factor[:, None, None]
        return mixing + new_column[..., None] * unit_column
    return lax.fori_loop(0, vector_count, gram_step, jnp.zeros_like(gram_matrix))

def combine(flat, mixing):
    highest = lax.Precision.HIGHEST
    widened = flat.astype(jnp.float32)
    flat_re = widened[:, 0]
    flat_im = widened[:, 1]
    mixing_re = mixing[:, 0]
    mixing_im = mixing[:, 1]
    result_re = jnp.einsum('nlk,nlr->nkr', mixing_re, flat_re, precision=highest) - jnp.einsum('nlk,nlr->nkr', mixing_im, flat_im, precision=highest)
    result_im = jnp.einsum('nlk,nlr->nkr', mixing_re, flat_im, precision=highest) + jnp.einsum('nlk,nlr->nkr', mixing_im, flat_re, precision=highest)
    return jnp.stack([result_re, result_im], axis=1)

def orthonormalize(vectors):
    extent = vectors.shape[-1]
    flat = vectors.reshape(vectors.shape[:3] + (-1,))
    mixing = coefficients(gram_of(flat), extent ** 3)
    return (combine(flat, mixing).reshape(vectors.shape), mixing)

def boundary_face(basis, position, layer):
    sliced = lax.index_in_dim(basis, layer, 5 + position, keepdims=False)
    return sliced.reshape(sliced.shape[:4] + (-1,))

def link_face(links, direction, layer):
    sliced = lax.index_in_dim(links[direction], layer, 3 + direction, keepdims=False)
    flat = sliced.reshape(sliced.shape[:3] + (-1,))
    return jnp.concatenate([flat, flat], axis=-1)

def apply_spin(matrix_re, matrix_im, value_re, value_im):
    halfway = value_re.shape[-1] // 2
    parts_re = [value_re[..., :halfway], value_re[..., halfway:]]
    parts_im = [value_im[..., :halfway], value_im[..., halfway:]]
    outs_re = []
    outs_im = []
    for row_spin in range(2):
        total_re = jnp.zeros_like(parts_re[0])
        total_im = jnp.zeros_like(parts_im[0])
        for col_spin in range(2):
            coef_re = float(matrix_re[row_spin, col_spin])
            coef_im = float(matrix_im[row_spin, col_spin])
            if coef_re != 0.0:
                total_re = total_re + coef_re * parts_re[col_spin]
                total_im = total_im + coef_re * parts_im[col_spin]
            if coef_im != 0.0:
                total_re = total_re - coef_im * parts_im[col_spin]
                total_im = total_im + coef_im * parts_re[col_spin]
        outs_re.append(total_re)
        outs_im.append(total_im)
    return (jnp.concatenate(outs_re, axis=-1), jnp.concatenate(outs_im, axis=-1))

def inner_block(left_re, left_im, right_re, right_im):
    highest = lax.Precision.HIGHEST
    count = left_re.shape[0]
    left_re = left_re.reshape(count, -1)
    left_im = left_im.reshape(count, -1)
    right_re = right_re.reshape(count, -1)
    right_im = right_im.reshape(count, -1)
    result_re = jnp.einsum('kr,lr->kl', left_re, right_re, precision=highest) + jnp.einsum('kr,lr->kl', left_im, right_im, precision=highest)
    result_im = jnp.einsum('kr,lr->kl', left_re, right_im, precision=highest) - jnp.einsum('kr,lr->kl', left_im, right_re, precision=highest)
    return (result_re, result_im)

def coarse_link(own_face, after_face, hopping, direction):
    after_re = after_face[:, 0][:, :, None]
    after_im = after_face[:, 1][:, :, None]
    link_re = hopping[0][None, None]
    link_im = hopping[1][None, None]
    moved_re = lax.optimization_barrier(jnp.sum(link_re * after_re, axis=3)) - lax.optimization_barrier(jnp.sum(link_im * after_im, axis=3))
    moved_im = lax.optimization_barrier(jnp.sum(link_re * after_im, axis=3)) + lax.optimization_barrier(jnp.sum(link_im * after_re, axis=3))
    matrix_re, matrix_im = spin_blocks()[direction]
    upper_re, upper_im = apply_spin(matrix_re, matrix_im, moved_re[1], moved_im[1])
    lower_re, lower_im = apply_spin(matrix_re.T, -matrix_im.T, moved_re[0], moved_im[0])
    own_re = own_face[:, 0]
    own_im = own_face[:, 1]
    same_zero = inner_block(own_re[0], own_im[0], moved_re[0], moved_im[0])
    same_one = inner_block(own_re[1], own_im[1], moved_re[1], moved_im[1])
    cross_up = inner_block(own_re[0], own_im[0], upper_re, upper_im)
    cross_down = inner_block(own_re[1], own_im[1], lower_re, lower_im)
    parts = []
    for member in range(2):
        top = jnp.concatenate([same_zero[member], -cross_up[member]], axis=1)
        bottom = jnp.concatenate([-cross_down[member], same_one[member]], axis=1)
        parts.append(jnp.concatenate([top, bottom], axis=0))
    return jnp.stack(parts)

def block_links(basis, far_faces, links):
    extent = basis.shape[-1]
    result = []
    for direction in range(4):
        own_face = boundary_face(basis, direction, extent - 1)
        hopping = link_face(links, direction, extent - 1)
        if direction < 3:
            after_face = far_faces[direction]
        else:
            after_face = -boundary_face(basis, 3, 0)
        result.append(coarse_link(own_face, after_face, hopping, direction))
    stacked = jnp.stack(result, axis=1)
    return stacked.reshape(2, -1)

def reference(near_null, gauge, site_map):
    extent = AGG
    blocks_x = NX // extent
    blocks_y = NY // extent
    blocks_z = NZ // extent
    block_count = blocks_x * blocks_y * blocks_z

    def to_blocks(packed):
        shaped = packed.reshape(blocks_x, extent, blocks_y, extent, blocks_z, extent, 2, -1)
        shaped = jnp.transpose(shaped, (0, 2, 4, 1, 3, 5, 6, 7))
        return shaped.reshape((block_count, extent, extent, extent, 2, -1))
    vector_blocks = to_blocks(near_null)
    gauge_blocks = to_blocks(gauge)

    def build(block):
        prolong, mixing = orthonormalize(chiral_layout(block))
        return prolong
    prolong = lax.map(build, vector_blocks)

    def neighbour(position):
        faces = jax.vmap(lambda basis: boundary_face(basis, position, 0))(prolong)
        faces = faces.reshape((blocks_x, blocks_y, blocks_z) + faces.shape[1:])
        faces = jnp.roll(faces, -1, axis=position)
        return faces.reshape((block_count,) + faces.shape[3:])
    after_x = neighbour(0)
    after_y = neighbour(1)
    after_z = neighbour(2)

    def per_block(inputs):
        basis, face_x, face_y, face_z, gauge_block = inputs
        return block_links(basis, [face_x, face_y, face_z], gauge_layout(gauge_block))
    coarse = lax.map(per_block, (prolong, after_x, after_y, after_z, gauge_blocks))
    coarse = coarse.reshape((blocks_x, blocks_y, blocks_z) + coarse.shape[1:])
    by_column = jnp.transpose(coarse, (2, 0, 1, 3, 4)).reshape(blocks_z, blocks_x * blocks_y, 2, -1)

    def arrange(entries, targets):
        return jnp.zeros_like(entries).at[targets].set(entries)
    return jax.vmap(arrange)(by_column, site_map)
```

```python
import jax
import jax.numpy as jnp
import numpy as np
from jax import lax
from jax.experimental import pallas as pl
from jax.experimental.pallas import tpu as pltpu
from jax.sharding import PartitionSpec as P

F32 = jnp.float32
BF16 = jnp.bfloat16
SITES = 64
FACE = 16
NVEC = 24
GROUPS = 12
WIDE = GROUPS * NVEC
PAD = 384
FULL = 4 * WIDE
LINKS = 144
COUNT = 32
TARGET = 64.0
FULL_PRECISION = lax.Precision.HIGHEST
GAMMA = [
    ((0, 1, -1j), (1, 0, -1j)),
    ((0, 1, -1), (1, 0, 1)),
    ((0, 0, -1j), (1, 1, 1j)),
    ((0, 0, 1), (1, 1, 1)),
]


def site_rows(axis, layer):
    rows = []
    for first in range(4):
        for second in range(4):
            place = [first, second]
            place.insert(axis, layer)
            rows.append(place[0] * 16 + place[1] * 4 + place[2])
    return rows


def row_selection():
    sites = []
    for part in range(2):
        sites += [2 * site + part for site in range(SITES)]
    for layer in (3, 0):
        for axis in range(3):
            for part in range(2):
                sites += [2 * site + part for site in site_rows(axis, layer)]
    chosen = np.zeros((len(sites), 2 * SITES), np.float32)
    chosen[np.arange(len(sites)), sites] = 1.0
    return chosen


def gram_fold():
    out = np.zeros((2, WIDE, 128), np.float32)
    for lane in range(WIDE):
        chirality, vector = lane // 144, lane % 24
        for part in range(2):
            out[part, lane, chirality * 48 + part * 24 + vector] = 1.0
    return out


def mixing_spread():
    out = np.zeros((128, 4, PAD), np.float32)
    for part in range(2):
        for chirality in range(2):
            for lane in range(144):
                source = chirality * 48 + part * 24 + lane % 24
                out[source, part * 2 + chirality, chirality * 144 + lane] = 1.0
    return out.reshape(128, 4 * PAD)


def colour_turns():
    out = np.zeros((WIDE, 2, PAD), np.float32)
    for lane in range(WIDE):
        base, colour, vector = lane // 72, lane // 24 % 3, lane % 24
        for turn in (1, 2):
            out[base * 72 + (colour + turn) % 3 * 24 + vector, turn - 1, lane] = 1.0
    return out.reshape(WIDE, 2 * PAD)


def link_spread():
    out = np.zeros((128, 3, PAD), np.float32)
    for lane in range(WIDE):
        colour = lane // 24 % 3
        for turn in range(3):
            out[colour * 3 + (colour + turn) % 3, turn, lane] = 1.0
    return out.reshape(128, 3 * PAD)


def link_pick():
    out = np.zeros((LINKS, 13, 128), np.float32)
    for piece in range(13):
        start = 9 * piece if piece < 12 else 135
        for entry in range(9):
            out[start + entry, piece, entry] = 1.0
    return out.reshape(LINKS, 13 * 128)


def dot(left, right, dims=((1,), (0,)), precision=None):
    return lax.dot_general(left, right, (dims, ((), ())), precision=precision, preferred_element_type=F32)


def time_rows(block):
    return jnp.concatenate([block[:, step * WIDE : (step + 1) * WIDE] for step in range(4)], axis=0)


def lane_of(shape):
    return lax.broadcasted_iota(jnp.int32, shape, 1)


def row_of(shape):
    return lax.broadcasted_iota(jnp.int32, shape, 0)


def mixing_rows(hermitian, hermitian_turned):
    shape = (NVEC, 128)
    lanes, rows = lane_of(shape), row_of(shape)
    lower = lanes < 48
    lower_row = lower[:1]
    mix = jnp.where((lanes % 48 == rows) & (lanes < 96), 1.0, 0.0)
    turned = jnp.where((lanes % 48 == rows + 24) & (lanes < 96), 1.0, 0.0)
    weights = jnp.ones(shape, F32)

    def spread(column, offset):
        first = hermitian[:, offset + column : offset + column + 1]
        second = hermitian[:, 48 + offset + column : 49 + offset + column]
        return jnp.where(lower, first, second)

    for column in range(NVEC):
        row = hermitian[column : column + 1]
        row_turned = hermitian_turned[column : column + 1]
        mix_row = mix[column : column + 1]
        mix_row_turned = turned[column : column + 1]
        product = row * mix_row
        first = jnp.sum(jnp.where(lower_row, product, 0.0), axis=1, keepdims=True)
        second = jnp.sum(jnp.where(lower_row, 0.0, product), axis=1, keepdims=True)
        weight = jnp.where(lower_row, first, second)
        weights = jnp.where(rows == column, weight, weights)
        if column == NVEC - 1:
            break
        ratio = jnp.where(rows > column, TARGET / weight, 0.0)
        by_re = spread(column, 0) * ratio
        by_im = spread(column, 24) * ratio
        hermitian, hermitian_turned = (
            hermitian - (by_re * row + by_im * row_turned),
            hermitian_turned - (by_re * row_turned - by_im * row),
        )
        mix, turned = (
            mix - (by_re * mix_row + by_im * mix_row_turned),
            turned - (by_re * mix_row_turned - by_im * mix_row),
        )
    return mix * jnp.sqrt(TARGET / weights)


def first_kernel(nn_ref, sel_ref, fold_ref, own_ref, start_ref, mix_ref, px_ref, py_ref, pz_ref):
    chosen = dot(sel_ref[...], nn_ref[...]).astype(BF16)
    every = chosen[:128]
    tall = time_rows(every)
    tall_re = time_rows(every[:64])
    tall_im = time_rows(every[64:])
    wide_re = dot(tall, tall, ((0,), (0,)))
    cross = dot(tall_re, tall_im, ((0,), (0,)))
    crossed = dot(tall_im, tall_re, ((0,), (0,)))
    wide_im = cross - crossed
    group = lane_of((NVEC, WIDE)) // NVEC
    fold_re = jnp.zeros((NVEC, WIDE), F32)
    fold_im = jnp.zeros((NVEC, WIDE), F32)
    for index in range(GROUPS):
        here = slice(index * NVEC, (index + 1) * NVEC)
        fold_re = jnp.where(group == index, wide_re[here], fold_re)
        fold_im = jnp.where(group == index, wide_im[here], fold_im)
    to_re = fold_ref[0]
    to_im = fold_ref[1]
    hermitian = dot(fold_re, to_re, precision=FULL_PRECISION) - dot(fold_im, to_im, precision=FULL_PRECISION)
    hermitian_turned = dot(fold_im, to_re, precision=FULL_PRECISION) + dot(fold_re, to_im, precision=FULL_PRECISION)
    mix = mixing_rows(hermitian, hermitian_turned)
    mix_ref[...] = mix
    parts = []
    rest = mix
    for _ in range(3):
        part = rest.astype(BF16).astype(F32)
        parts.append(part)
        rest = rest - part
    nothing = jnp.zeros((8, 128), F32)
    packed = [part[:16] for part in parts] + [jnp.concatenate([part[16:], nothing], axis=0) for part in parts]
    for axis, out in enumerate((px_ref, py_ref, pz_ref)):
        first = 224 + 32 * axis
        out[:32, :] = chosen[first : first + 32]
        for index, piece in enumerate(packed):
            out[32:, index * 128 : (index + 1) * 128] = piece.astype(BF16)
        out[32:, 768:] = jnp.zeros((16, 384), BF16)
    for axis in range(3):
        first = 128 + 32 * axis
        own_ref[axis, :64] = time_rows(chosen[first : first + 16])
        own_ref[axis, 64:] = time_rows(chosen[first + 16 : first + 32])
    own_ref[3] = every[:, 3 * WIDE :]
    start_ref[...] = every[:, :WIDE]


def second_kernel(
    rx_ref, ry_ref, rz_ref, own_ref, start_ref, mix_ref, ga_ref, sel_ref, pick_ref, links_ref, turns_ref, spread_ref,
    code_ref, flat_ref, order_ref,
):
    face_links = dot(sel_ref[:224], ga_ref[...]).astype(BF16)
    picked = dot(face_links, pick_ref[...]).astype(BF16)
    link_rows = []
    for axis in range(3):
        first = 128 + 32 * axis
        for part in range(2):
            for step in range(4):
                piece = axis * 4 + step
                link_rows.append(picked[first + 16 * part : first + 16 * part + 16, piece * 128 : (piece + 1) * 128])
    link_rows.append(picked[:128, 12 * 128 :])
    gauge = dot(jnp.concatenate(link_rows, axis=0), links_ref[...])
    ahead = []
    for ref in (rx_ref, ry_ref, rz_ref):
        ahead.append(time_rows(ref[:16, :]))
        ahead.append(time_rows(ref[16:32, :]))
    ahead.append(start_ref[...])
    ahead = jnp.concatenate(ahead, axis=0)
    turned = dot(ahead, turns_ref[...])
    same = ahead.astype(F32)
    shifted = [same, turned[:, :WIDE], turned[:, PAD : PAD + WIDE]]
    mixings = []
    for ref in (rx_ref, ry_ref, rz_ref):
        total = jnp.zeros((NVEC, 128), F32)
        for index in (2, 1, 0):
            low = ref[32:48, index * 128 : (index + 1) * 128].astype(F32)
            high = ref[32:48, (index + 3) * 128 : (index + 4) * 128].astype(F32)[:8]
            total = total + jnp.concatenate([low, high], axis=0)
        mixings.append(total)
    mixings.append(mix_ref[...])
    spread = dot(jnp.concatenate(mixings, axis=0), spread_ref[...], precision=FULL_PRECISION)
    own_mix = mix_ref[...]
    group = lane_of((NVEC, WIDE)) // NVEC
    halves = []
    for direction in range(4):
        base = direction * 128
        sign = -1.0 if direction == 3 else 1.0
        moved_re = jnp.zeros((64, WIDE), F32)
        moved_im = jnp.zeros((64, WIDE), F32)
        for turn in range(3):
            lanes = slice(turn * PAD, turn * PAD + WIDE)
            u_re = gauge[base : base + 64, lanes]
            u_im = gauge[base + 64 : base + 128, lanes]
            v_re = shifted[turn][base : base + 64]
            v_im = shifted[turn][base + 64 : base + 128]
            moved_re = moved_re + (u_re * v_re - u_im * v_im)
            moved_im = moved_im + (u_re * v_im + u_im * v_re)
        if sign < 0:
            moved_re, moved_im = -moved_re, -moved_im
        top_re = moved_re.astype(BF16)
        top_im = moved_im.astype(BF16)
        low_re = (moved_re - top_re.astype(F32)).astype(BF16)
        low_im = (moved_im - top_im.astype(F32)).astype(BF16)
        mine = own_ref[direction]
        mine = jnp.concatenate([mine, mine], axis=0)
        wide_re = dot(mine, jnp.concatenate([top_re, top_im, low_re, low_im], axis=0), ((0,), (0,)))
        wide_im = dot(mine, jnp.concatenate([top_im, -top_re, low_im, -low_re], axis=0), ((0,), (0,)))
        fold_re, fold_im = [], []
        for chirality in range(2):
            sum_re = jnp.zeros((NVEC, WIDE), F32)
            sum_im = jnp.zeros((NVEC, WIDE), F32)
            for row_spin, col_spin, value in GAMMA[direction]:
                if chirality == 1:
                    row_spin, col_spin, value = col_spin, row_spin, np.conj(value)
                factor = -value
                for colour in range(3):
                    index = chirality * 6 + row_spin * 3 + colour
                    here = slice(index * NVEC, (index + 1) * NVEC)
                    at_re, at_im = wide_re[here], wide_im[here]
                    if np.imag(factor) != 0:
                        over_re, over_im = -float(np.imag(factor)) * at_im, float(np.imag(factor)) * at_re
                    else:
                        over_re, over_im = float(np.real(factor)) * at_re, float(np.real(factor)) * at_im
                    partner = (1 - chirality) * 6 + col_spin * 3 + colour
                    sum_re = jnp.where(group == index, at_re, jnp.where(group == partner, over_re, sum_re))
                    sum_im = jnp.where(group == index, at_im, jnp.where(group == partner, over_im, sum_im))
            fold_re.append(sum_re)
            fold_im.append(sum_im)
        folded = jnp.concatenate(fold_re + fold_im, axis=0)
        rows = slice(direction * NVEC, (direction + 1) * NVEC)
        mix_re = jnp.concatenate([spread[rows, :WIDE], spread[rows, PAD : PAD + WIDE]], axis=0)
        mix_im = jnp.concatenate([spread[rows, 2 * PAD : 2 * PAD + WIDE], spread[rows, 3 * PAD : 3 * PAD + WIDE]], axis=0)
        by_re = dot(folded, mix_re, ((1,), (1,)), FULL_PRECISION)
        by_im = dot(folded, mix_im, ((1,), (1,)), FULL_PRECISION)
        halves.append((by_re[:48] - by_im[48:], by_im[:48] + by_re[48:]))
    square = (NVEC, 48)
    zero = jnp.zeros((NVEC, NVEC), F32)
    left_re = jnp.concatenate(
        [jnp.concatenate([own_mix[:, 0:24], zero], axis=1), jnp.concatenate([zero, own_mix[:, 48:72]], axis=1)], axis=0
    )
    left_im = jnp.concatenate(
        [jnp.concatenate([own_mix[:, 24:48], zero], axis=1), jnp.concatenate([zero, own_mix[:, 72:96]], axis=1)], axis=0
    )
    left = jnp.concatenate([left_re, left_im], axis=0)
    for direction in range(4):
        half_re, half_im = halves[direction]
        on_re = dot(left, half_re, precision=FULL_PRECISION)
        on_im = dot(left, half_im, precision=FULL_PRECISION)
        flat_ref[direction * 96 : direction * 96 + 48, :] = on_re[:48] + on_im[48:]
        flat_ref[direction * 96 + 48 : direction * 96 + 96, :] = on_im[:48] - on_re[48:]
    pieces = [flat_ref[pl.ds(row, 48, stride=8), :] for row in range(8)]
    long = jnp.concatenate(pieces, axis=1)
    for direction in range(4):
        for part in range(2):
            first = (direction * 2 + part) * 6
            for third in range(3):
                target = direction * 36 + third * 2 + part
                order_ref[pl.ds(target, 6, stride=6), :] = long[first : first + 6, third * 128 : (third + 1) * 128]
    powers = []
    for block in range(9):
        values = order_ref[block * 16 : block * 16 + 16, :]
        largest = jnp.max(jnp.abs(values), axis=0, keepdims=True)
        power = jnp.clip(jnp.ceil(jnp.log2(jnp.maximum(largest, 1e-30)) + 1e-3), -100.0, 120.0)
        scaled = values * jnp.exp2(-power) * 32767.0
        scaled = jnp.clip(jnp.round(scaled), -32767.0, 32767.0)
        code_ref[block * 16 : block * 16 + 16, :] = scaled.astype(jnp.int32).astype(jnp.int16)
        powers.append(power)
    powers = jnp.concatenate(powers + [jnp.zeros((7, 128), F32)], axis=0)
    code_ref[144:160, :] = powers.astype(jnp.int32).astype(jnp.int16)


def place_kernel(order, site_ref, code_ref, out_ref):
    for index in range(COUNT):
        target = site_ref[0, order[index]]
        power = code_ref[index, 144:160, :].astype(jnp.int32).astype(F32)
        scale = jnp.exp2(power) * (1.0 / 32767.0)
        for block in range(9):
            values = code_ref[index, block * 16 : block * 16 + 16, :].astype(jnp.int32).astype(F32)
            out_ref[target, block * 16 : block * 16 + 16, :] = values * scale[block : block + 1]


def first_call(block, selection):
    return pl.pallas_call(
        first_kernel,
        out_shape=[
            jax.ShapeDtypeStruct((4, 128, WIDE), BF16),
            jax.ShapeDtypeStruct((128, WIDE), BF16),
            jax.ShapeDtypeStruct((NVEC, 128), F32),
        ]
        + [jax.ShapeDtypeStruct((48, FULL), BF16)] * 3,
        compiler_params=pltpu.CompilerParams(vmem_limit_bytes=40 * 2**20),
        name="gram_and_mixing",
    )(block, selection, jnp.asarray(gram_fold(), F32))


def second_call(faces, own, start, mix, gauge, selection):
    return pl.pallas_call(
        second_kernel,
        out_shape=jax.ShapeDtypeStruct((160, 128), jnp.int16),
        scratch_shapes=[pltpu.VMEM((384, 48), F32), pltpu.VMEM((144, 128), F32)],
        compiler_params=pltpu.CompilerParams(vmem_limit_bytes=40 * 2**20),
        name="coarse_links",
    )(
        *faces, own, start, mix, gauge, selection,
        jnp.asarray(link_pick(), BF16), jnp.asarray(link_spread(), BF16), jnp.asarray(colour_turns(), BF16),
        jnp.asarray(mixing_spread(), F32),
    )


def place_call(site_map, codes, order):
    return pl.pallas_call(
        lambda site_ref, code_ref, out_ref: place_kernel(order, site_ref, code_ref, out_ref),
        in_specs=[pl.BlockSpec(memory_space=pltpu.SMEM), pl.BlockSpec(memory_space=pltpu.VMEM)],
        out_shape=jax.ShapeDtypeStruct((COUNT, 144, 128), F32),
        compiler_params=pltpu.CompilerParams(vmem_limit_bytes=40 * 2**20),
        name="place_links",
    )(site_map, codes)


def passed_back(value, axis):
    count = lax.axis_size(axis)
    return lax.ppermute(value, axis, [(source, (source - 1) % count) for source in range(count)])


def ring_order():
    return [(z % 4) * 8 + (z // 4) * 2 + core for z in range(16) for core in range(2)]


def body(near_null, gauge, site_map):
    selection = jnp.asarray(row_selection(), BF16)
    own, start, mix, *faces = first_call(near_null.reshape(2 * SITES, FULL), selection)
    faces = [passed_back(face, axis) for face, axis in zip(faces, ("gx", "gy", "zt"))]
    code = second_call(faces, own, start, mix, gauge.reshape(2 * SITES, LINKS), selection)
    order = ring_order()
    codes = lax.all_gather(code[None], ("gx", "gy"), axis=0, tiled=True, axis_index_groups=[order])
    placed = place_call(site_map, codes, order)
    placed = placed.reshape(COUNT, 72, 2, 128).transpose(0, 2, 1, 3)
    return placed.reshape(1, COUNT, 2, 9216)


def solution(mesh):
    return jax.shard_map(
        body,
        mesh=mesh,
        in_specs=(P("gx", "gy", "zt", None, None), P("gx", "gy", "zt", None, None), P("zt", None)),
        out_specs=P("zt", None, None, None),
        check_vma=False,
    )
```

```python
import jax
import jax.numpy as jnp
import numpy as np
from jax import lax
from jax.experimental import pallas as pl
from jax.experimental.pallas import tpu as pltpu
from jax.sharding import PartitionSpec as P

F32 = jnp.float32
BF16 = jnp.bfloat16
SITES = 64
FACE = 16
NVEC = 24
GROUPS = 12
WIDE = GROUPS * NVEC
PAD = 384
FULL = 4 * WIDE
LINKS = 144
COUNT = 32
MIX_ROW = 288
SENT = 368
TARGET = 64.0
FULL_PRECISION = lax.Precision.HIGHEST
GAMMA = [
    ((0, 1, -1j), (1, 0, -1j)),
    ((0, 1, -1), (1, 0, 1)),
    ((0, 0, -1j), (1, 1, 1j)),
    ((0, 0, 1), (1, 1, 1)),
]


def dot(left, right, dims=((1,), (0,)), precision=None):
    return lax.dot_general(left, right, (dims, ((), ())), precision=precision, preferred_element_type=F32)


def time_rows(block):
    return jnp.concatenate([block[:, step * WIDE : (step + 1) * WIDE] for step in range(4)], axis=0)


def lane_of(shape):
    return lax.broadcasted_iota(jnp.int32, shape, 1)


def row_of(shape):
    return lax.broadcasted_iota(jnp.int32, shape, 0)


def ones_where(condition, dtype):
    return jnp.where(condition, 1.0, 0.0).astype(dtype)


def all_rows():
    shape = (SITES, 2 * SITES)
    first = lane_of(shape) - 2 * row_of(shape)
    return [ones_where(first == part, BF16) for part in range(2)]


def layer_rows(layer):
    shape = (FACE, 2 * SITES)
    lanes, rows = lane_of(shape), row_of(shape)
    sites = [layer * 16 + rows, (rows // 4) * 16 + layer * 4 + rows % 4, rows * 4 + layer]
    return [ones_where(lanes == 2 * site + part, BF16) for site in sites for part in range(2)]


def gram_fold():
    shape = (WIDE, 128)
    rows = row_of(shape)
    away = lane_of(shape) - ((rows // 144) * 48 + rows % NVEC)
    return jnp.concatenate([ones_where(away == part * NVEC, F32) for part in range(2)], axis=1)


def mixing_spread():
    shape = (128, PAD)
    lanes, rows = lane_of(shape), row_of(shape)
    blocks = []
    for part in range(2):
        for chirality in range(2):
            inside = (lanes >= chirality * 144) & (lanes < chirality * 144 + 144)
            source = jnp.where(inside, lanes % NVEC + chirality * 48 + part * NVEC, -1)
            blocks.append(ones_where(rows == source, F32))
    return jnp.concatenate(blocks, axis=1)


def colour_turns():
    shape = (WIDE, PAD)
    lanes, rows = lane_of(shape), row_of(shape)
    colour = (lanes // NVEC) % 3
    blocks = []
    for turn in (1, 2):
        source = lanes + NVEC * jnp.where(colour + turn >= 3, turn - 3, turn)
        blocks.append(ones_where((rows == source) & (lanes < WIDE), BF16))
    return jnp.concatenate(blocks, axis=1)


def link_spread():
    shape = (16, PAD)
    lanes, rows = lane_of(shape), row_of(shape)
    colour = (lanes // NVEC) % 3
    blocks = []
    for turn in range(3):
        source = colour * 3 + (colour + turn) % 3
        blocks.append(ones_where((rows == source) & (lanes < WIDE), BF16))
    return jnp.concatenate(blocks, axis=1)


def link_pick():
    shape = (LINKS, 128)
    lanes = lane_of(shape)
    start = jnp.where(lanes < 9, row_of(shape) - lanes, -1)
    starts = [9 * piece for piece in range(12)] + [135]
    return jnp.concatenate([ones_where(start == first, BF16) for first in starts], axis=1)


def mixing_rows(hermitian, hermitian_turned):
    shape = (NVEC, 128)
    lanes, rows = lane_of(shape), row_of(shape)
    lower = lanes < 48
    lower_row = lower[:1]
    mix = jnp.where((lanes % 48 == rows) & (lanes < 96), 1.0, 0.0)
    turned = jnp.where((lanes % 48 == rows + 24) & (lanes < 96), 1.0, 0.0)
    weights = jnp.ones(shape, F32)

    def spread(column, offset):
        first = hermitian[:, offset + column : offset + column + 1]
        second = hermitian[:, 48 + offset + column : 49 + offset + column]
        return jnp.where(lower, first, second)

    for column in range(NVEC):
        row = hermitian[column : column + 1]
        row_turned = hermitian_turned[column : column + 1]
        mix_row = mix[column : column + 1]
        mix_row_turned = turned[column : column + 1]
        product = row * mix_row
        first = jnp.sum(jnp.where(lower_row, product, 0.0), axis=1, keepdims=True)
        second = jnp.sum(jnp.where(lower_row, 0.0, product), axis=1, keepdims=True)
        weight = jnp.where(lower_row, first, second)
        weights = jnp.where(rows == column, weight, weights)
        if column == NVEC - 1:
            break
        ratio = jnp.where(rows > column, TARGET / weight, 0.0)
        by_re = spread(column, 0) * ratio
        by_im = spread(column, 24) * ratio
        hermitian, hermitian_turned = (
            hermitian - (by_re * row + by_im * row_turned),
            hermitian_turned - (by_re * row_turned - by_im * row),
        )
        mix, turned = (
            mix - (by_re * mix_row + by_im * mix_row_turned),
            turned - (by_re * mix_row_turned - by_im * mix_row),
        )
    return mix * jnp.sqrt(TARGET / weights)


def first_kernel(nn_ref, own_ref, start_ref, mix_ref, py_ref, px_ref, pz_ref):
    selection = jnp.concatenate(all_rows() + layer_rows(3) + layer_rows(0), axis=0)
    chosen = dot(selection, nn_ref[...]).astype(BF16)
    every = chosen[:128]
    tall = time_rows(every)
    tall_turned = time_rows(jnp.concatenate([every[64:], -every[:64]], axis=0))
    wide_re = dot(tall, tall, ((0,), (0,)))
    wide_im = dot(tall, tall_turned, ((0,), (0,)))
    group = lane_of((NVEC, WIDE)) // NVEC
    fold_re = jnp.zeros((NVEC, WIDE), F32)
    fold_im = jnp.zeros((NVEC, WIDE), F32)
    for index in range(GROUPS):
        here = slice(index * NVEC, (index + 1) * NVEC)
        fold_re = jnp.where(group == index, wide_re[here], fold_re)
        fold_im = jnp.where(group == index, wide_im[here], fold_im)
    folded = dot(jnp.concatenate([fold_re, fold_im], axis=0), gram_fold(), precision=FULL_PRECISION)
    hermitian = folded[:NVEC, :128] - folded[NVEC:, 128:]
    hermitian_turned = folded[NVEC:, :128] + folded[:NVEC, 128:]
    mix = mixing_rows(hermitian, hermitian_turned)
    mix_ref[...] = mix
    parts = []
    rest = mix
    for _ in range(3):
        part = rest.astype(BF16).astype(F32)
        parts.append(part)
        rest = rest - part
    packed = jnp.concatenate(parts + [jnp.zeros((8, 128), F32)], axis=0).astype(BF16)
    for axis, out in enumerate((px_ref, py_ref, pz_ref)):
        first = 224 + 32 * axis
        for column in range(9):
            out[column * 32 : column * 32 + 32, :] = chosen[first : first + 32, column * 128 : (column + 1) * 128]
        out[MIX_ROW:, :] = packed
    for axis in range(3):
        first = 128 + 32 * axis
        own_ref[axis, :64] = time_rows(chosen[first : first + 16])
        own_ref[axis, 64:] = time_rows(chosen[first + 16 : first + 32])
    own_ref[3] = every[:, 3 * WIDE :]
    start_ref[...] = every[:, :WIDE]


def second_kernel(
    rx_ref, ry_ref, rz_ref, own_ref, start_ref, mix_ref, ga_ref, code_ref, flat_ref, order_ref
):
    selection = jnp.concatenate(all_rows() + layer_rows(3), axis=0)
    face_links = dot(selection, ga_ref[...]).astype(BF16)
    picked = dot(face_links, link_pick()).astype(BF16)
    link_rows = []
    for axis in range(3):
        first = 128 + 32 * axis
        for part in range(2):
            for step in range(4):
                piece = axis * 4 + step
                link_rows.append(picked[first + 16 * part : first + 16 * part + 16, piece * 128 : piece * 128 + 16])
    link_rows.append(picked[:128, 12 * 128 : 12 * 128 + 16])
    gauge = dot(jnp.concatenate(link_rows, axis=0), link_spread())
    ahead = []
    for ref in (rx_ref, ry_ref, rz_ref):
        face = jnp.concatenate([ref[column * 32 : column * 32 + 32, :] for column in range(9)], axis=1)
        ahead.append(time_rows(face[:16]))
        ahead.append(time_rows(face[16:]))
    ahead.append(start_ref[...])
    ahead = jnp.concatenate(ahead, axis=0)
    turned = dot(ahead, colour_turns())
    same = ahead.astype(F32)
    shifted = [same, turned[:, :WIDE], turned[:, PAD : PAD + WIDE]]
    mixings = []
    for ref in (rx_ref, ry_ref, rz_ref):
        parts = ref[MIX_ROW:SENT, :].astype(F32)
        mixings.append(parts[48:72] + parts[24:48] + parts[:24])
    mixings.append(mix_ref[...])
    spread = dot(jnp.concatenate(mixings, axis=0), mixing_spread(), precision=FULL_PRECISION)
    own_mix = mix_ref[...]
    group = lane_of((NVEC, WIDE)) // NVEC
    halves = []
    for direction in range(4):
        base = direction * 128
        sign = -1.0 if direction == 3 else 1.0
        moved_re = jnp.zeros((64, WIDE), F32)
        moved_im = jnp.zeros((64, WIDE), F32)
        for turn in range(3):
            lanes = slice(turn * PAD, turn * PAD + WIDE)
            u_re = gauge[base : base + 64, lanes]
            u_im = gauge[base + 64 : base + 128, lanes]
            v_re = shifted[turn][base : base + 64]
            v_im = shifted[turn][base + 64 : base + 128]
            moved_re = moved_re + (u_re * v_re - u_im * v_im)
            moved_im = moved_im + (u_re * v_im + u_im * v_re)
        if sign < 0:
            moved_re, moved_im = -moved_re, -moved_im
        top_re = moved_re.astype(BF16)
        top_im = moved_im.astype(BF16)
        low_re = (moved_re - top_re.astype(F32)).astype(BF16)
        low_im = (moved_im - top_im.astype(F32)).astype(BF16)
        mine = own_ref[direction]
        mine = jnp.concatenate([mine, mine], axis=0)
        wide_re = dot(mine, jnp.concatenate([top_re, top_im, low_re, low_im], axis=0), ((0,), (0,)))
        wide_im = dot(mine, jnp.concatenate([top_im, -top_re, low_im, -low_re], axis=0), ((0,), (0,)))
        fold_re, fold_im = [], []
        for chirality in range(2):
            sum_re = jnp.zeros((NVEC, WIDE), F32)
            sum_im = jnp.zeros((NVEC, WIDE), F32)
            for row_spin, col_spin, value in GAMMA[direction]:
                if chirality == 1:
                    row_spin, col_spin, value = col_spin, row_spin, np.conj(value)
                factor = -value
                for colour in range(3):
                    index = chirality * 6 + row_spin * 3 + colour
                    here = slice(index * NVEC, (index + 1) * NVEC)
                    at_re, at_im = wide_re[here], wide_im[here]
                    if np.imag(factor) != 0:
                        over_re, over_im = -float(np.imag(factor)) * at_im, float(np.imag(factor)) * at_re
                    else:
                        over_re, over_im = float(np.real(factor)) * at_re, float(np.real(factor)) * at_im
                    partner = (1 - chirality) * 6 + col_spin * 3 + colour
                    sum_re = jnp.where(group == index, at_re, jnp.where(group == partner, over_re, sum_re))
                    sum_im = jnp.where(group == index, at_im, jnp.where(group == partner, over_im, sum_im))
            fold_re.append(sum_re)
            fold_im.append(sum_im)
        folded = jnp.concatenate(fold_re + fold_im, axis=0)
        rows = slice(direction * NVEC, (direction + 1) * NVEC)
        mix_re = jnp.concatenate([spread[rows, :WIDE], spread[rows, PAD : PAD + WIDE]], axis=0)
        mix_im = jnp.concatenate([spread[rows, 2 * PAD : 2 * PAD + WIDE], spread[rows, 3 * PAD : 3 * PAD + WIDE]], axis=0)
        by_re = dot(folded, mix_re, ((1,), (1,)), FULL_PRECISION)
        by_im = dot(folded, mix_im, ((1,), (1,)), FULL_PRECISION)
        halves.append((by_re[:48] - by_im[48:], by_im[:48] + by_re[48:]))
    square = (NVEC, 48)
    zero = jnp.zeros((NVEC, NVEC), F32)
    left_re = jnp.concatenate(
        [jnp.concatenate([own_mix[:, 0:24], zero], axis=1), jnp.concatenate([zero, own_mix[:, 48:72]], axis=1)], axis=0
    )
    left_im = jnp.concatenate(
        [jnp.concatenate([own_mix[:, 24:48], zero], axis=1), jnp.concatenate([zero, own_mix[:, 72:96]], axis=1)], axis=0
    )
    left = jnp.concatenate([left_re, left_im], axis=0)
    for direction in range(4):
        half_re, half_im = halves[direction]
        on_re = dot(left, half_re, precision=FULL_PRECISION)
        on_im = dot(left, half_im, precision=FULL_PRECISION)
        flat_ref[direction * 96 : direction * 96 + 48, :] = on_re[:48] + on_im[48:]
        flat_ref[direction * 96 + 48 : direction * 96 + 96, :] = on_im[:48] - on_re[48:]
    pieces = [flat_ref[pl.ds(row, 48, stride=8), :] for row in range(8)]
    long = jnp.concatenate(pieces, axis=1)
    for direction in range(4):
        for part in range(2):
            first = (direction * 2 + part) * 6
            for third in range(3):
                target = direction * 36 + third * 2 + part
                order_ref[pl.ds(target, 6, stride=6), :] = long[first : first + 6, third * 128 : (third + 1) * 128]
    powers = []
    for block in range(9):
        values = order_ref[block * 16 : block * 16 + 16, :]
        largest = jnp.max(jnp.abs(values), axis=0, keepdims=True)
        power = jnp.clip(jnp.ceil(jnp.log2(jnp.maximum(largest, 1e-30)) + 1e-3), -100.0, 120.0)
        scaled = values * jnp.exp2(-power) * 32767.0
        scaled = jnp.clip(jnp.round(scaled), -32767.0, 32767.0)
        code_ref[block * 16 : block * 16 + 16, :] = scaled.astype(jnp.int32).astype(jnp.int16)
        powers.append(power)
    powers = jnp.concatenate(powers + [jnp.zeros((7, 128), F32)], axis=0)
    code_ref[144:160, :] = powers.astype(jnp.int32).astype(jnp.int16)


def place_kernel(order, site_ref, code_ref, out_ref):
    for index in range(COUNT):
        target = site_ref[0, order[index]]
        power = code_ref[index, 144:160, :].astype(jnp.int32).astype(F32)
        scale = jnp.exp2(power) * (1.0 / 32767.0)
        for block in range(9):
            values = code_ref[index, block * 16 : block * 16 + 16, :].astype(jnp.int32).astype(F32)
            out_ref[target, block * 16 : block * 16 + 16, :] = values * scale[block : block + 1]


def first_call(block):
    return pl.pallas_call(
        first_kernel,
        out_shape=[
            jax.ShapeDtypeStruct((4, 128, WIDE), BF16),
            jax.ShapeDtypeStruct((128, WIDE), BF16),
            jax.ShapeDtypeStruct((NVEC, 128), F32),
        ]
        + [jax.ShapeDtypeStruct((SENT, 128), BF16)] * 3,
        compiler_params=pltpu.CompilerParams(vmem_limit_bytes=40 * 2**20),
        name="gram_and_mixing",
    )(block)


def second_call(faces, own, start, mix, gauge):
    return pl.pallas_call(
        second_kernel,
        out_shape=jax.ShapeDtypeStruct((160, 128), jnp.int16),
        scratch_shapes=[pltpu.VMEM((384, 48), F32), pltpu.VMEM((144, 128), F32)],
        compiler_params=pltpu.CompilerParams(vmem_limit_bytes=40 * 2**20),
        name="coarse_links",
    )(*faces, own, start, mix, gauge)


def place_call(site_map, codes, order):
    return pl.pallas_call(
        lambda site_ref, code_ref, out_ref: place_kernel(order, site_ref, code_ref, out_ref),
        in_specs=[pl.BlockSpec(memory_space=pltpu.SMEM), pl.BlockSpec(memory_space=pltpu.VMEM)],
        out_shape=jax.ShapeDtypeStruct((COUNT, 144, 128), F32),
        compiler_params=pltpu.CompilerParams(vmem_limit_bytes=40 * 2**20),
        name="place_links",
    )(site_map, codes)


def passed_back(value, axis):
    count = lax.axis_size(axis)
    return lax.ppermute(value, axis, [(source, (source - 1) % count) for source in range(count)])


def flat_index(z, core):
    return (z % 4) * 8 + (z // 4) * 2 + core


def gathered(code):
    pairs = [[flat_index(z, core), flat_index(z + 1, core)] for z in range(0, 16, 2) for core in range(2)]
    rings = [[flat_index(z + odd, core) for z in range(0, 16, 2) for core in range(2)] for odd in range(2)]
    names = ("gx", "gy")
    code = lax.all_gather(code[None], names, axis=0, tiled=True, axis_index_groups=pairs)
    code = lax.all_gather(code, names, axis=0, tiled=True, axis_index_groups=rings)
    return code, [index for pair in pairs for index in pair]


def body(near_null, gauge, site_map):
    own, start, mix, face_y, face_x, face_z = first_call(near_null.reshape(2 * SITES, FULL))
    face_y = passed_back(face_y, "gy")
    face_x = passed_back(face_x, "gx")
    face_z = passed_back(face_z, "zt")
    code = second_call((face_x, face_y, face_z), own, start, mix, gauge.reshape(2 * SITES, LINKS))
    codes, order = gathered(code)
    placed = place_call(site_map, codes, order)
    placed = placed.reshape(COUNT, 72, 2, 128).transpose(0, 2, 1, 3)
    return placed.reshape(1, COUNT, 2, 9216)


def solution(mesh):
    return jax.shard_map(
        body,
        mesh=mesh,
        in_specs=(P("gx", "gy", "zt", None, None), P("gx", "gy", "zt", None, None), P("zt", None)),
        out_specs=P("zt", None, None, None),
        check_vma=False,
    )
```

```python
import jax
import jax.numpy as jnp
import numpy as np
from jax import lax
from jax.experimental import pallas as pl
from jax.experimental.pallas import tpu as pltpu
from jax.sharding import PartitionSpec as P

F32 = jnp.float32
BF16 = jnp.bfloat16
SITES = 64
FACE = 16
NVEC = 24
GROUPS = 12
WIDE = GROUPS * NVEC
PAD = 384
FULL = 4 * WIDE
LINKS = 144
COUNT = 32
MIX_ROW = 288
SENT = 368
TARGET = 64.0
FULL_PRECISION = lax.Precision.HIGHEST
GAMMA = [
    ((0, 1, -1j), (1, 0, -1j)),
    ((0, 1, -1), (1, 0, 1)),
    ((0, 0, -1j), (1, 1, 1j)),
    ((0, 0, 1), (1, 1, 1)),
]


def dot(left, right, dims=((1,), (0,)), precision=None):
    return lax.dot_general(left, right, (dims, ((), ())), precision=precision, preferred_element_type=F32)


def time_rows(block):
    return jnp.concatenate([block[:, step * WIDE : (step + 1) * WIDE] for step in range(4)], axis=0)


def lane_of(shape):
    return lax.broadcasted_iota(jnp.int32, shape, 1)


def row_of(shape):
    return lax.broadcasted_iota(jnp.int32, shape, 0)


def ones_where(condition, dtype):
    return jnp.where(condition, 1.0, 0.0).astype(dtype)


def all_rows():
    shape = (SITES, 2 * SITES)
    first = lane_of(shape) - 2 * row_of(shape)
    return [ones_where(first == part, BF16) for part in range(2)]


def layer_rows(layer):
    shape = (FACE, 2 * SITES)
    lanes, rows = lane_of(shape), row_of(shape)
    sites = [layer * 16 + rows, (rows // 4) * 16 + layer * 4 + rows % 4, rows * 4 + layer]
    return [ones_where(lanes == 2 * site + part, BF16) for site in sites for part in range(2)]


def gram_fold():
    shape = (WIDE, 128)
    rows = row_of(shape)
    away = lane_of(shape) - ((rows // 144) * 48 + rows % NVEC)
    return jnp.concatenate([ones_where(away == part * NVEC, F32) for part in range(2)], axis=1)


def mixing_spread():
    shape = (128, PAD)
    lanes, rows = lane_of(shape), row_of(shape)
    blocks = []
    for part in range(2):
        for chirality in range(2):
            inside = (lanes >= chirality * 144) & (lanes < chirality * 144 + 144)
            source = jnp.where(inside, lanes % NVEC + chirality * 48 + part * NVEC, -1)
            blocks.append(ones_where(rows == source, F32))
    return jnp.concatenate(blocks, axis=1)


def colour_turns():
    shape = (WIDE, PAD)
    lanes, rows = lane_of(shape), row_of(shape)
    colour = (lanes // NVEC) % 3
    blocks = []
    for turn in (1, 2):
        source = lanes + NVEC * jnp.where(colour + turn >= 3, turn - 3, turn)
        blocks.append(ones_where((rows == source) & (lanes < WIDE), BF16))
    return jnp.concatenate(blocks, axis=1)


def link_spread():
    shape = (16, PAD)
    lanes, rows = lane_of(shape), row_of(shape)
    colour = (lanes // NVEC) % 3
    blocks = []
    for turn in range(3):
        source = colour * 3 + (colour + turn) % 3
        blocks.append(ones_where((rows == source) & (lanes < WIDE), BF16))
    return jnp.concatenate(blocks, axis=1)


def link_pick():
    shape = (LINKS, 128)
    lanes = lane_of(shape)
    start = jnp.where(lanes < 9, row_of(shape) - lanes, -1)
    starts = [9 * piece for piece in range(12)] + [135]
    return jnp.concatenate([ones_where(start == first, BF16) for first in starts], axis=1)


def mixing_rows(hermitian, hermitian_turned):
    shape = (8, 128)
    lanes, rows = lane_of(shape), row_of(shape)
    lower = lanes < 48
    blocks = range(3)

    def split(value):
        return [value[8 * block : 8 * block + 8] for block in blocks]

    gram, gram_turned = split(hermitian), split(hermitian_turned)
    mix = [jnp.where((lanes % 48 == rows + 8 * block) & (lanes < 96), 1.0, 0.0) for block in blocks]
    turned = [jnp.where((lanes % 48 == rows + 8 * block + 24) & (lanes < 96), 1.0, 0.0) for block in blocks]
    weights = []

    def spread(value, at):
        return jnp.where(lower, value[:, at : at + 1], value[:, 48 + at : 49 + at])

    for column in range(NVEC):
        own, place = column // 8, column % 8
        here = slice(place, place + 1)
        row, row_turned = gram[own][here], gram_turned[own][here]
        mix_row, mix_turned = mix[own][here], turned[own][here]
        product = row * mix_row
        both = jnp.concatenate([jnp.where(lower[:1], product, 0.0), jnp.where(lower[:1], 0.0, product)], axis=0)
        both = jnp.sum(both, axis=1, keepdims=True)
        weight = jnp.where(lower[:1], both[:1], both[1:])
        weights.append(weight)
        active = [block for block in blocks if 8 * block + 7 > column]
        if not active:
            break
        ratio = TARGET / weight
        for block in active:
            a_re, a_im = spread(gram[block], column), spread(gram[block], column + 24)
            scale = jnp.where(rows + 8 * block > column, ratio, 0.0) if block == own else ratio
            gram_step = a_re * row + a_im * row_turned
            gram_turned_step = a_re * row_turned - a_im * row
            mix_step = a_re * mix_row + a_im * mix_turned
            turned_step = a_re * mix_turned - a_im * mix_row
            gram[block] = gram[block] - scale * gram_step
            gram_turned[block] = gram_turned[block] - scale * gram_turned_step
            mix[block] = mix[block] - scale * mix_step
            turned[block] = turned[block] - scale * turned_step
    weights = jnp.concatenate(weights, axis=0)
    return jnp.concatenate(mix, axis=0) * jnp.sqrt(TARGET / weights)


def first_kernel(nn_ref, own_ref, start_ref, mix_ref, py_ref, px_ref, pz_ref):
    selection = jnp.concatenate(all_rows() + layer_rows(3) + layer_rows(0), axis=0)
    chosen = dot(selection, nn_ref[...]).astype(BF16)
    every = chosen[:128]
    tall = time_rows(every)
    tall_turned = time_rows(jnp.concatenate([every[64:], -every[:64]], axis=0))
    wide_re = dot(tall, tall, ((0,), (0,)))
    wide_im = dot(tall, tall_turned, ((0,), (0,)))
    group = lane_of((NVEC, WIDE)) // NVEC
    fold_re = jnp.zeros((NVEC, WIDE), F32)
    fold_im = jnp.zeros((NVEC, WIDE), F32)
    for index in range(GROUPS):
        here = slice(index * NVEC, (index + 1) * NVEC)
        fold_re = jnp.where(group == index, wide_re[here], fold_re)
        fold_im = jnp.where(group == index, wide_im[here], fold_im)
    folded = dot(jnp.concatenate([fold_re, fold_im], axis=0), gram_fold(), precision=FULL_PRECISION)
    hermitian = folded[:NVEC, :128] - folded[NVEC:, 128:]
    hermitian_turned = folded[NVEC:, :128] + folded[:NVEC, 128:]
    mix = mixing_rows(hermitian, hermitian_turned)
    mix_ref[...] = mix
    parts = []
    rest = mix
    for _ in range(3):
        part = rest.astype(BF16).astype(F32)
        parts.append(part)
        rest = rest - part
    packed = jnp.concatenate(parts + [jnp.zeros((8, 128), F32)], axis=0).astype(BF16)
    for axis, out in enumerate((px_ref, py_ref, pz_ref)):
        first = 224 + 32 * axis
        for column in range(9):
            out[column * 32 : column * 32 + 32, :] = chosen[first : first + 32, column * 128 : (column + 1) * 128]
        out[MIX_ROW:, :] = packed
    for axis in range(3):
        first = 128 + 32 * axis
        own_ref[axis, :64] = time_rows(chosen[first : first + 16])
        own_ref[axis, 64:] = time_rows(chosen[first + 16 : first + 32])
    own_ref[3] = every[:, 3 * WIDE :]
    start_ref[...] = every[:, :WIDE]


def hop(gauge, same, turned, sign):
    moved_re = jnp.zeros((64, WIDE), F32)
    moved_im = jnp.zeros((64, WIDE), F32)
    for turn in range(3):
        u = gauge[:, turn * PAD : turn * PAD + WIDE].astype(F32)
        v = same.astype(F32) if turn == 0 else turned[:, (turn - 1) * PAD : (turn - 1) * PAD + WIDE]
        moved_re = moved_re + (u[:64] * v[:64] - u[64:] * v[64:])
        moved_im = moved_im + (u[:64] * v[64:] + u[64:] * v[:64])
    if sign < 0:
        moved_re, moved_im = -moved_re, -moved_im
    top_re, top_im = moved_re.astype(BF16), moved_im.astype(BF16)
    low_re = (moved_re - top_re.astype(F32)).astype(BF16)
    low_im = (moved_im - top_im.astype(F32)).astype(BF16)
    return (
        jnp.concatenate([top_re, top_im, low_re, low_im], axis=0),
        jnp.concatenate([top_im, -top_re, low_im, -low_re], axis=0),
    )


def spin_fold(wide_re, wide_im, direction):
    group = lane_of((NVEC, WIDE)) // NVEC
    fold_re, fold_im = [], []
    for chirality in range(2):
        sum_re = jnp.zeros((NVEC, WIDE), F32)
        sum_im = jnp.zeros((NVEC, WIDE), F32)
        for row_spin, col_spin, value in GAMMA[direction]:
            if chirality == 1:
                row_spin, col_spin, value = col_spin, row_spin, np.conj(value)
            factor = -value
            for colour in range(3):
                index = chirality * 6 + row_spin * 3 + colour
                here = slice(index * NVEC, (index + 1) * NVEC)
                at_re, at_im = wide_re[here], wide_im[here]
                if np.imag(factor) != 0:
                    over_re, over_im = -float(np.imag(factor)) * at_im, float(np.imag(factor)) * at_re
                else:
                    over_re, over_im = float(np.real(factor)) * at_re, float(np.real(factor)) * at_im
                partner = (1 - chirality) * 6 + col_spin * 3 + colour
                sum_re = jnp.where(group == index, at_re, jnp.where(group == partner, over_re, sum_re))
                sum_im = jnp.where(group == index, at_im, jnp.where(group == partner, over_im, sum_im))
        fold_re.append(sum_re)
        fold_im.append(sum_im)
    return jnp.concatenate(fold_re + fold_im, axis=0)


def link_matrix(folded, spread, left):
    mix_re = jnp.concatenate([spread[:, :WIDE], spread[:, PAD : PAD + WIDE]], axis=0)
    mix_im = jnp.concatenate([spread[:, 2 * PAD : 2 * PAD + WIDE], spread[:, 3 * PAD : 3 * PAD + WIDE]], axis=0)
    by_re = dot(folded, mix_re, ((1,), (1,)), FULL_PRECISION)
    by_im = dot(folded, mix_im, ((1,), (1,)), FULL_PRECISION)
    on_re = dot(left, by_re[:48] - by_im[48:], precision=FULL_PRECISION)
    on_im = dot(left, by_im[:48] + by_re[48:], precision=FULL_PRECISION)
    return on_re[:48] + on_im[48:], on_im[:48] - on_re[48:]


def own_kernel(own_ref, start_ref, mix_ref, ga_ref, gauge_ref, turns_ref, spread_ref, rows_ref, left_ref, last_ref):
    selection = jnp.concatenate(all_rows() + layer_rows(3), axis=0)
    face_links = dot(selection, ga_ref[...]).astype(BF16)
    picked = dot(face_links, link_pick()).astype(BF16)
    link_rows = []
    for axis in range(3):
        first = 128 + 32 * axis
        for part in range(2):
            for step in range(4):
                piece = axis * 4 + step
                link_rows.append(picked[first + 16 * part : first + 16 * part + 16, piece * 128 : piece * 128 + 16])
    link_rows.append(picked[:128, 12 * 128 : 12 * 128 + 16])
    gauge = dot(jnp.concatenate(link_rows, axis=0), link_spread()).astype(BF16)
    gauge_ref[...] = gauge[:384]
    turns = colour_turns()
    turns_ref[...] = turns
    spread_matrix = mixing_spread()
    spread_ref[...] = spread_matrix
    mix = mix_ref[...]
    zero = jnp.zeros((NVEC, NVEC), F32)
    left = []
    for part in range(2):
        first = mix[:, part * 24 : part * 24 + 24]
        second = mix[:, 48 + part * 24 : 72 + part * 24]
        left += [jnp.concatenate([first, zero], axis=1), jnp.concatenate([zero, second], axis=1)]
    left = jnp.concatenate(left, axis=0)
    left_ref[...] = left
    for axis in range(3):
        mine = own_ref[axis]
        rows_ref[axis] = jnp.concatenate([mine, mine], axis=0).T
    mine = own_ref[3]
    rows = jnp.concatenate([mine, mine], axis=0).T
    start = start_ref[...]
    to_re, to_im = hop(gauge[384:], start, dot(start, turns), -1.0)
    folded = spin_fold(dot(rows, to_re), dot(rows, to_im), 3)
    spread = dot(mix, spread_matrix, precision=FULL_PRECISION)
    last_re, last_im = link_matrix(folded, spread, left)
    last_ref[:48, :] = last_re
    last_ref[48:, :] = last_im


def second_kernel(
    rx_ref, ry_ref, rz_ref, gauge_ref, turns_ref, spread_ref, rows_ref, left_ref, last_ref, code_ref, flat_ref, order_ref
):
    flat_ref[288:, :] = last_ref[...]
    left = left_ref[...]
    mixings = []
    for ref in (rx_ref, ry_ref, rz_ref):
        parts = ref[MIX_ROW:SENT, :].astype(F32)
        mixings.append(parts[48:72] + parts[24:48] + parts[:24])
    spread = dot(jnp.concatenate(mixings, axis=0), spread_ref[...], precision=FULL_PRECISION)
    for direction, ref in enumerate((rx_ref, ry_ref, rz_ref)):
        face = jnp.concatenate([ref[column * 32 : column * 32 + 32, :] for column in range(9)], axis=1)
        ahead = jnp.concatenate([time_rows(face[:16]), time_rows(face[16:])], axis=0)
        turned = dot(ahead, turns_ref[...])
        base = direction * 128
        to_re, to_im = hop(gauge_ref[base : base + 128, :], ahead, turned, 1.0)
        rows = rows_ref[direction]
        folded = spin_fold(dot(rows, to_re), dot(rows, to_im), direction)
        y_re, y_im = link_matrix(folded, spread[direction * NVEC : (direction + 1) * NVEC], left)
        flat_ref[direction * 96 : direction * 96 + 48, :] = y_re
        flat_ref[direction * 96 + 48 : direction * 96 + 96, :] = y_im
    pieces = [flat_ref[pl.ds(row, 48, stride=8), :] for row in range(8)]
    long = jnp.concatenate(pieces, axis=1)
    for direction in range(4):
        for part in range(2):
            first = (direction * 2 + part) * 6
            for third in range(3):
                target = direction * 36 + third * 2 + part
                order_ref[pl.ds(target, 6, stride=6), :] = long[first : first + 6, third * 128 : (third + 1) * 128]
    powers = []
    for block in range(9):
        values = order_ref[block * 16 : block * 16 + 16, :]
        largest = jnp.max(jnp.abs(values), axis=0, keepdims=True)
        power = jnp.clip(jnp.ceil(jnp.log2(jnp.maximum(largest, 1e-30)) + 1e-3), -100.0, 120.0)
        scaled = values * jnp.exp2(-power) * 32767.0
        scaled = jnp.clip(jnp.round(scaled), -32767.0, 32767.0)
        code_ref[block * 16 : block * 16 + 16, :] = scaled.astype(jnp.int32).astype(jnp.int16)
        powers.append(power)
    powers = jnp.concatenate(powers + [jnp.zeros((7, 128), F32)], axis=0)
    code_ref[144:160, :] = powers.astype(jnp.int32).astype(jnp.int16)


def place_kernel(order, site_ref, code_ref, out_ref, wide_ref, sem_ref):
    copies = []
    for index in range(COUNT):
        power = code_ref[index, 144:160, :].astype(jnp.int32).astype(F32)
        scale = jnp.exp2(power) * (1.0 / 32767.0)
        for block in range(9):
            values = code_ref[index, block * 16 : block * 16 + 16, :].astype(jnp.int32).astype(F32)
            wide_ref[index, block * 16 : block * 16 + 16, :] = values * scale[block : block + 1]
        target = site_ref[0, order[index]]
        copy = pltpu.make_async_copy(wide_ref.at[index], out_ref.at[target], sem_ref.at[index])
        copy.start()
        copies.append(copy)
    for copy in copies:
        copy.wait()


def first_call(block):
    return pl.pallas_call(
        first_kernel,
        out_shape=[
            jax.ShapeDtypeStruct((4, 128, WIDE), BF16),
            jax.ShapeDtypeStruct((128, WIDE), BF16),
            jax.ShapeDtypeStruct((NVEC, 128), F32),
        ]
        + [jax.ShapeDtypeStruct((SENT, 128), BF16)] * 3,
        compiler_params=pltpu.CompilerParams(vmem_limit_bytes=40 * 2**20),
        name="gram_and_mixing",
    )(block)


def own_call(own, start, mix, gauge):
    return pl.pallas_call(
        own_kernel,
        out_shape=[
            jax.ShapeDtypeStruct((384, 3 * PAD), BF16),
            jax.ShapeDtypeStruct((WIDE, 2 * PAD), BF16),
            jax.ShapeDtypeStruct((128, 4 * PAD), F32),
            jax.ShapeDtypeStruct((3, WIDE, 256), BF16),
            jax.ShapeDtypeStruct((96, 48), F32),
            jax.ShapeDtypeStruct((96, 48), F32),
        ],
        compiler_params=pltpu.CompilerParams(vmem_limit_bytes=40 * 2**20),
        cost_estimate=pl.CostEstimate(flops=2 * 10**9, bytes_accessed=4 * 10**6, transcendentals=0),
        name="own_part",
    )(own, start, mix, gauge)


def second_call(faces, prepared):
    return pl.pallas_call(
        second_kernel,
        out_shape=jax.ShapeDtypeStruct((160, 128), jnp.int16),
        scratch_shapes=[pltpu.VMEM((384, 48), F32), pltpu.VMEM((144, 128), F32)],
        compiler_params=pltpu.CompilerParams(vmem_limit_bytes=40 * 2**20),
        name="coarse_links",
    )(*faces, *prepared)


def place_call(site_map, codes, order):
    return pl.pallas_call(
        lambda *refs: place_kernel(order, *refs),
        in_specs=[pl.BlockSpec(memory_space=pltpu.SMEM), pl.BlockSpec(memory_space=pltpu.VMEM)],
        out_specs=pl.BlockSpec(memory_space=pl.ANY),
        out_shape=jax.ShapeDtypeStruct((COUNT, 144, 128), F32),
        scratch_shapes=[pltpu.VMEM((COUNT, 144, 128), F32), pltpu.SemaphoreType.DMA((COUNT,))],
        compiler_params=pltpu.CompilerParams(vmem_limit_bytes=40 * 2**20),
        name="place_links",
    )(site_map, codes)


def passed_back(value, axis):
    count = lax.axis_size(axis)
    return lax.ppermute(value, axis, [(source, (source - 1) % count) for source in range(count)])


def flat_index(z, core):
    return (z % 4) * 8 + (z // 4) * 2 + core


def gathered(code):
    pairs = [[flat_index(z, core), flat_index(z + 1, core)] for z in range(0, 16, 2) for core in range(2)]
    rings = [[flat_index(z + odd, core) for z in range(0, 16, 2) for core in range(2)] for odd in range(2)]
    names = ("gx", "gy")
    code = lax.all_gather(code[None], names, axis=0, tiled=True, axis_index_groups=pairs)
    code = lax.all_gather(code, names, axis=0, tiled=True, axis_index_groups=rings)
    return code, [index for pair in pairs for index in pair]


def body(near_null, gauge, site_map):
    own, start, mix, face_y, face_x, face_z = first_call(near_null.reshape(2 * SITES, FULL))
    face_y = passed_back(face_y, "gy")
    face_x = passed_back(face_x, "gx")
    face_z = passed_back(face_z, "zt")
    prepared = own_call(own, start, mix, gauge.reshape(2 * SITES, LINKS))
    code = second_call((face_x, face_y, face_z), prepared)
    codes, order = gathered(code)
    placed = place_call(site_map, codes, order)
    placed = placed.reshape(COUNT, 72, 2, 128).transpose(0, 2, 1, 3)
    return placed.reshape(1, COUNT, 2, 9216)


def solution(mesh):
    return jax.shard_map(
        body,
        mesh=mesh,
        in_specs=(P("gx", "gy", "zt", None, None), P("gx", "gy", "zt", None, None), P("zt", None)),
        out_specs=P("zt", None, None, None),
        check_vma=False,
    )
```

```python
import jax
import jax.numpy as jnp
import numpy as np
from jax import lax
from jax.experimental import pallas as pl
from jax.experimental.pallas import tpu as pltpu
from jax.sharding import PartitionSpec as P

F32 = jnp.float32
BF16 = jnp.bfloat16
SITES = 64
FACE = 16
NVEC = 24
GROUPS = 12
WIDE = GROUPS * NVEC
PAD = 384
FULL = 4 * WIDE
LINKS = 144
COUNT = 32
CHUNK = 4
MIX_ROW = 288
SENT = 336
TARGET = 64.0
GAMMA = [
    ((0, 1, -1j), (1, 0, -1j)),
    ((0, 1, -1), (1, 0, 1)),
    ((0, 0, -1j), (1, 1, 1j)),
    ((0, 0, 1), (1, 1, 1)),
]


def dot(left, right, dims=((1,), (0,))):
    return lax.dot_general(left, right, (dims, ((), ())), preferred_element_type=F32)


def bf16_parts(value, count):
    parts = []
    for _ in range(count):
        part = value.astype(BF16)
        parts.append(part)
        value = value - part.astype(F32)
    return parts


def dot_parts(parts, ones):
    rows = parts[0].shape[0]
    out = dot(jnp.concatenate(parts, axis=0), ones)
    total = out[(len(parts) - 1) * rows :]
    for index in reversed(range(len(parts) - 1)):
        total = total + out[index * rows : (index + 1) * rows]
    return total


def time_rows(block):
    return jnp.concatenate([block[:, step * WIDE : (step + 1) * WIDE] for step in range(4)], axis=0)


def lane_of(shape):
    return lax.broadcasted_iota(jnp.int32, shape, 1)


def row_of(shape):
    return lax.broadcasted_iota(jnp.int32, shape, 0)


def ones_where(condition, dtype):
    return jnp.where(condition, 1.0, 0.0).astype(dtype)


def all_rows():
    shape = (SITES, 2 * SITES)
    first = lane_of(shape) - 2 * row_of(shape)
    return [ones_where(first == part, BF16) for part in range(2)]


def layer_rows(layer):
    shape = (FACE, 2 * SITES)
    lanes, rows = lane_of(shape), row_of(shape)
    sites = [layer * 16 + rows, (rows // 4) * 16 + layer * 4 + rows % 4, rows * 4 + layer]
    return [ones_where(lanes == 2 * site + part, BF16) for site in sites for part in range(2)]


def gram_fold():
    shape = (WIDE, 128)
    rows = row_of(shape)
    away = lane_of(shape) - ((rows // 144) * 48 + rows % NVEC)
    return jnp.concatenate([ones_where(away == part * NVEC, BF16) for part in range(2)], axis=1)


def mixing_spread():
    shape = (128, PAD)
    lanes, rows = lane_of(shape), row_of(shape)
    blocks = []
    for part in range(2):
        for chirality in range(2):
            inside = (lanes >= chirality * 144) & (lanes < chirality * 144 + 144)
            source = jnp.where(inside, lanes % NVEC + chirality * 48 + part * NVEC, -1)
            blocks.append(ones_where(rows == source, BF16))
    return jnp.concatenate(blocks, axis=1)


def colour_turns():
    shape = (WIDE, PAD)
    lanes, rows = lane_of(shape), row_of(shape)
    colour = (lanes // NVEC) % 3
    blocks = []
    for turn in (1, 2):
        source = lanes + NVEC * jnp.where(colour + turn >= 3, turn - 3, turn)
        blocks.append(ones_where((rows == source) & (lanes < WIDE), BF16))
    return jnp.concatenate(blocks, axis=1)


def link_spread():
    shape = (16, PAD)
    lanes, rows = lane_of(shape), row_of(shape)
    colour = (lanes // NVEC) % 3
    blocks = []
    for turn in range(3):
        source = colour * 3 + (colour + turn) % 3
        blocks.append(ones_where((rows == source) & (lanes < WIDE), BF16))
    return jnp.concatenate(blocks, axis=1)


def link_pick():
    shape = (LINKS, 128)
    lanes = lane_of(shape)
    start = jnp.where(lanes < 9, row_of(shape) - lanes, -1)
    starts = [9 * piece for piece in range(12)] + [135]
    return jnp.concatenate([ones_where(start == first, BF16) for first in starts], axis=1)


def mixing_rows(hermitian, hermitian_turned):
    shape = (8, 128)
    lanes, rows = lane_of(shape), row_of(shape)
    lower = lanes < 48
    blocks = range(3)

    def split(value):
        return [value[8 * block : 8 * block + 8] for block in blocks]

    gram, gram_turned = split(hermitian), split(hermitian_turned)
    mix = [jnp.where((lanes % 48 == rows + 8 * block) & (lanes < 96), 1.0, 0.0) for block in blocks]
    turned = [jnp.where((lanes % 48 == rows + 8 * block + 24) & (lanes < 96), 1.0, 0.0) for block in blocks]
    weights = []

    def spread(value, at):
        return jnp.where(lower, value[:, at : at + 1], value[:, 48 + at : 49 + at])

    for column in range(NVEC):
        own, place = column // 8, column % 8
        here = slice(place, place + 1)
        row, row_turned = gram[own][here], gram_turned[own][here]
        mix_row, mix_turned = mix[own][here], turned[own][here]
        product = row * mix_row
        both = jnp.concatenate([jnp.where(lower[:1], product, 0.0), jnp.where(lower[:1], 0.0, product)], axis=0)
        both = jnp.sum(both, axis=1, keepdims=True)
        weight = jnp.where(lower[:1], both[:1], both[1:])
        weights.append(weight)
        active = [block for block in blocks if 8 * block + 7 > column]
        if not active:
            break
        ratio = TARGET / weight
        for block in active:
            a_re, a_im = spread(gram[block], column), spread(gram[block], column + 24)
            scale = jnp.where(rows + 8 * block > column, ratio, 0.0) if block == own else ratio
            gram_step = a_re * row + a_im * row_turned
            gram_turned_step = a_re * row_turned - a_im * row
            mix_step = a_re * mix_row + a_im * mix_turned
            turned_step = a_re * mix_turned - a_im * mix_row
            gram[block] = gram[block] - scale * gram_step
            gram_turned[block] = gram_turned[block] - scale * gram_turned_step
            mix[block] = mix[block] - scale * mix_step
            turned[block] = turned[block] - scale * turned_step
    weights = jnp.concatenate(weights, axis=0)
    return jnp.concatenate(mix, axis=0) * jnp.sqrt(TARGET / weights)


def first_kernel(nn_ref, own_ref, start_ref, mix_ref, py_ref, px_ref, pz_ref):
    selection = jnp.concatenate(all_rows() + layer_rows(3) + layer_rows(0), axis=0)
    chosen = dot(selection, nn_ref[...]).astype(BF16)
    every = chosen[:128]
    tall = time_rows(every)
    tall_turned = time_rows(jnp.concatenate([every[64:], -every[:64]], axis=0))
    wide_re = dot(tall, tall, ((0,), (0,)))
    wide_im = dot(tall, tall_turned, ((0,), (0,)))
    group = lane_of((NVEC, WIDE)) // NVEC
    fold_re = jnp.zeros((NVEC, WIDE), F32)
    fold_im = jnp.zeros((NVEC, WIDE), F32)
    for index in range(GROUPS):
        here = slice(index * NVEC, (index + 1) * NVEC)
        fold_re = jnp.where(group == index, wide_re[here], fold_re)
        fold_im = jnp.where(group == index, wide_im[here], fold_im)
    folded = dot_parts(bf16_parts(jnp.concatenate([fold_re, fold_im], axis=0), 3), gram_fold())
    hermitian = folded[:NVEC, :128] - folded[NVEC:, 128:]
    hermitian_turned = folded[NVEC:, :128] + folded[:NVEC, 128:]
    mix = mixing_rows(hermitian, hermitian_turned)
    mix_ref[...] = mix
    packed = jnp.concatenate(bf16_parts(mix, 2), axis=0)
    for axis, out in enumerate((px_ref, py_ref, pz_ref)):
        first = 224 + 32 * axis
        for column in range(9):
            out[column * 32 : column * 32 + 32, :] = chosen[first : first + 32, column * 128 : (column + 1) * 128]
        out[MIX_ROW:, :] = packed
    for axis in range(3):
        first = 128 + 32 * axis
        own_ref[axis, :64] = time_rows(chosen[first : first + 16])
        own_ref[axis, 64:] = time_rows(chosen[first + 16 : first + 32])
    own_ref[3] = every[:, 3 * WIDE :]
    start_ref[...] = every[:, :WIDE]


def hop(gauge, same, turned, sign):
    moved_re = jnp.zeros((64, WIDE), F32)
    moved_im = jnp.zeros((64, WIDE), F32)
    for turn in range(3):
        u = gauge[:, turn * PAD : turn * PAD + WIDE].astype(F32)
        v = same.astype(F32) if turn == 0 else turned[:, (turn - 1) * PAD : (turn - 1) * PAD + WIDE]
        moved_re = moved_re + (u[:64] * v[:64] - u[64:] * v[64:])
        moved_im = moved_im + (u[:64] * v[64:] + u[64:] * v[:64])
    if sign < 0:
        moved_re, moved_im = -moved_re, -moved_im
    top_re, top_im = moved_re.astype(BF16), moved_im.astype(BF16)
    low_re = (moved_re - top_re.astype(F32)).astype(BF16)
    low_im = (moved_im - top_im.astype(F32)).astype(BF16)
    return (
        jnp.concatenate([top_re, top_im, low_re, low_im], axis=0),
        jnp.concatenate([top_im, -top_re, low_im, -low_re], axis=0),
    )


def spin_fold(wide_re, wide_im, direction):
    group = lane_of((NVEC, WIDE)) // NVEC
    fold_re, fold_im = [], []
    for chirality in range(2):
        sum_re = jnp.zeros((NVEC, WIDE), F32)
        sum_im = jnp.zeros((NVEC, WIDE), F32)
        for row_spin, col_spin, value in GAMMA[direction]:
            if chirality == 1:
                row_spin, col_spin, value = col_spin, row_spin, np.conj(value)
            factor = -value
            for colour in range(3):
                index = chirality * 6 + row_spin * 3 + colour
                here = slice(index * NVEC, (index + 1) * NVEC)
                at_re, at_im = wide_re[here], wide_im[here]
                if np.imag(factor) != 0:
                    over_re, over_im = -float(np.imag(factor)) * at_im, float(np.imag(factor)) * at_re
                else:
                    over_re, over_im = float(np.real(factor)) * at_re, float(np.real(factor)) * at_im
                partner = (1 - chirality) * 6 + col_spin * 3 + colour
                sum_re = jnp.where(group == index, at_re, jnp.where(group == partner, over_re, sum_re))
                sum_im = jnp.where(group == index, at_im, jnp.where(group == partner, over_im, sum_im))
        fold_re.append(sum_re)
        fold_im.append(sum_im)
    return jnp.concatenate(fold_re + fold_im, axis=0)


def spread_mixing(parts, ones):
    rows = parts[0].shape[0]
    out = dot(jnp.concatenate(parts, axis=0), ones).astype(BF16)
    gap = jnp.zeros((80, WIDE), BF16)
    result = []
    for first in range(0, rows, NVEC):
        pair = []
        for index in range(2):
            here = slice(index * rows + first, index * rows + first + NVEC)
            blocks = [out[here, block * PAD : block * PAD + WIDE] for block in range(4)]
            pair.append(jnp.concatenate([blocks[0], blocks[1], gap, blocks[2], blocks[3]], axis=0))
        result.append(pair)
    return result


def link_matrix(folded, mixing, left):
    top, low = bf16_parts(folded, 2)
    by = dot(jnp.concatenate([top, low], axis=0), mixing[0], ((1,), (1,)))
    by = by[:96] + (by[96:] + dot(top, mixing[1], ((1,), (1,))))
    by_re, by_im = by[:, :48], by[:, 128:]
    half = jnp.concatenate([by_re[:48] - by_im[48:], jnp.zeros((48, 80), F32), by_im[:48] + by_re[48:]], axis=1)
    top, low = bf16_parts(half, 2)
    on = dot(left, top)
    on = on[:96] + (on[96:] + dot(left[:96], low))
    return on[:48, :48] + on[48:, 128:], on[:48, 128:] - on[48:, :48]


def next_face(ref):
    face = jnp.concatenate([ref[column * 32 : column * 32 + 32, :] for column in range(9)], axis=1)
    parts = ref[MIX_ROW:SENT, :].astype(F32)
    parts = [parts[:NVEC].astype(BF16), parts[NVEC:].astype(BF16)]
    return jnp.concatenate([time_rows(face[:16]), time_rows(face[16:])], axis=0), parts


def write_rows(links, flat_ref, order_ref):
    count = 12 * len(links)
    for index, (_, matrix_re, matrix_im) in enumerate(links):
        flat_ref[index * 96 : index * 96 + 48, :] = matrix_re
        flat_ref[index * 96 + 48 : index * 96 + 96, :] = matrix_im
    long = jnp.concatenate([flat_ref[pl.ds(row, count, stride=8), :] for row in range(8)], axis=1)
    for index, (direction, _, _) in enumerate(links):
        for part in range(2):
            first = (index * 2 + part) * 6
            for third in range(3):
                target = direction * 36 + third * 2 + part
                order_ref[pl.ds(target, 6, stride=6), :] = long[first : first + 6, third * 128 : (third + 1) * 128]


def own_kernel(
    rx_ref, own_ref, start_ref, mix_ref, ga_ref, gauge_ref, turns_ref, spread_ref, rows_ref, left_ref, order_ref, flat_ref
):
    selection = jnp.concatenate(all_rows() + layer_rows(3), axis=0)
    face_links = dot(selection, ga_ref[...]).astype(BF16)
    picked = dot(face_links, link_pick()).astype(BF16)
    link_rows = []
    for axis in range(3):
        first = 128 + 32 * axis
        for part in range(2):
            for step in range(4):
                piece = axis * 4 + step
                link_rows.append(picked[first + 16 * part : first + 16 * part + 16, piece * 128 : piece * 128 + 16])
    link_rows.append(picked[:128, 12 * 128 : 12 * 128 + 16])
    gauge = dot(jnp.concatenate(link_rows, axis=0), link_spread()).astype(BF16)
    gauge_ref[...] = gauge[128:384]
    turns = colour_turns()
    turns_ref[...] = turns
    spread_matrix = mixing_spread()
    spread_ref[...] = spread_matrix
    mix = mix_ref[...]
    zero = jnp.zeros((NVEC, NVEC), F32)
    left = []
    for part in range(2):
        first = mix[:, part * 24 : part * 24 + 24]
        second = mix[:, 48 + part * 24 : 72 + part * 24]
        left += [jnp.concatenate([first, zero], axis=1), jnp.concatenate([zero, second], axis=1)]
    left = jnp.concatenate(bf16_parts(jnp.concatenate(left, axis=0), 2), axis=0)
    left_ref[...] = left
    rows = []
    for axis in range(4):
        mine = own_ref[axis]
        rows.append(jnp.concatenate([mine, mine], axis=0).T)
    rows_ref[0] = rows[1]
    rows_ref[1] = rows[2]
    face, mix_x = next_face(rx_ref)
    ahead = jnp.concatenate([face, start_ref[...]], axis=0)
    turned = dot(ahead, turns)
    mixings = spread_mixing([jnp.concatenate(pair, axis=0) for pair in zip(mix_x, bf16_parts(mix, 2))], spread_matrix)
    links = []
    for index, direction in enumerate((0, 3)):
        here = slice(index * 128, index * 128 + 128)
        to_re, to_im = hop(gauge[direction * 128 : direction * 128 + 128], ahead[here], turned[here], 1.0 - 2.0 * index)
        folded = spin_fold(dot(rows[direction], to_re), dot(rows[direction], to_im), direction)
        links.append((direction, *link_matrix(folded, mixings[index], left)))
    order_ref[...] = jnp.zeros((144, 128), F32)
    write_rows(links, flat_ref, order_ref)


def second_kernel(
    ry_ref, rz_ref, gauge_ref, turns_ref, spread_ref, rows_ref, left_ref, start_ref, code_ref, flat_ref, order_ref
):
    order_ref[...] = start_ref[...]
    left = left_ref[...]
    face_y, mix_y = next_face(ry_ref)
    face_z, mix_z = next_face(rz_ref)
    ahead = jnp.concatenate([face_y, face_z], axis=0)
    turned = dot(ahead, turns_ref[...])
    mixings = spread_mixing([jnp.concatenate(pair, axis=0) for pair in zip(mix_y, mix_z)], spread_ref[...])
    links = []
    for index, direction in enumerate((1, 2)):
        here = slice(index * 128, index * 128 + 128)
        to_re, to_im = hop(gauge_ref[here, :], ahead[here], turned[here], 1.0)
        rows = rows_ref[index]
        folded = spin_fold(dot(rows, to_re), dot(rows, to_im), direction)
        links.append((direction, *link_matrix(folded, mixings[index], left)))
    write_rows(links, flat_ref, order_ref)
    powers = []
    for block in range(9):
        values = order_ref[block * 16 : block * 16 + 16, :]
        largest = jnp.max(jnp.abs(values), axis=0, keepdims=True)
        power = jnp.clip(jnp.ceil(jnp.log2(jnp.maximum(largest, 1e-30)) + 1e-3), -100.0, 120.0)
        scaled = values * jnp.exp2(-power) * 32767.0
        scaled = jnp.clip(jnp.round(scaled), -32767.0, 32767.0)
        code_ref[block * 16 : block * 16 + 16, :] = scaled.astype(jnp.int32).astype(jnp.int16)
        powers.append(power)
    powers = jnp.concatenate(powers + [jnp.zeros((7, 128), F32)], axis=0)
    code_ref[144:160, :] = powers.astype(jnp.int32).astype(jnp.int16)


def place_kernel(order, site_ref, code_ref, out_ref, wide_ref, source_ref, sem_ref):
    for index in range(COUNT):
        source_ref[site_ref[0, order[index]]] = index
    copies = []
    for site in range(COUNT):
        source = source_ref[site]
        power = code_ref[source, 144:160, :].astype(jnp.int32).astype(F32)
        scale = jnp.exp2(power) * (1.0 / 32767.0)
        for block in range(9):
            values = code_ref[source, block * 16 : block * 16 + 16, :].astype(jnp.int32).astype(F32)
            wide_ref[site, block * 16 : block * 16 + 16, :] = values * scale[block : block + 1]
        if site % CHUNK == CHUNK - 1:
            here = pl.ds(site - CHUNK + 1, CHUNK)
            copy = pltpu.make_async_copy(wide_ref.at[here], out_ref.at[here], sem_ref.at[site // CHUNK])
            copy.start()
            copies.append(copy)
    for copy in copies:
        copy.wait()


def first_call(block):
    return pl.pallas_call(
        first_kernel,
        out_shape=[
            jax.ShapeDtypeStruct((4, 128, WIDE), BF16),
            jax.ShapeDtypeStruct((128, WIDE), BF16),
            jax.ShapeDtypeStruct((NVEC, 128), F32),
        ]
        + [jax.ShapeDtypeStruct((SENT, 128), BF16)] * 3,
        compiler_params=pltpu.CompilerParams(vmem_limit_bytes=40 * 2**20),
        name="gram_and_mixing",
    )(block)


def own_call(face_x, own, start, mix, gauge):
    return pl.pallas_call(
        own_kernel,
        out_shape=[
            jax.ShapeDtypeStruct((256, 3 * PAD), BF16),
            jax.ShapeDtypeStruct((WIDE, 2 * PAD), BF16),
            jax.ShapeDtypeStruct((128, 4 * PAD), BF16),
            jax.ShapeDtypeStruct((2, WIDE, 256), BF16),
            jax.ShapeDtypeStruct((192, 48), BF16),
            jax.ShapeDtypeStruct((144, 128), F32),
        ],
        scratch_shapes=[pltpu.VMEM((192, 48), F32)],
        compiler_params=pltpu.CompilerParams(vmem_limit_bytes=40 * 2**20),
        cost_estimate=pl.CostEstimate(flops=2 * 10**9, bytes_accessed=4 * 10**6, transcendentals=0),
        name="own_part",
    )(face_x, own, start, mix, gauge)


def second_call(face_y, face_z, prepared):
    return pl.pallas_call(
        second_kernel,
        out_shape=jax.ShapeDtypeStruct((160, 128), jnp.int16),
        scratch_shapes=[pltpu.VMEM((192, 48), F32), pltpu.VMEM((144, 128), F32)],
        compiler_params=pltpu.CompilerParams(vmem_limit_bytes=40 * 2**20),
        name="coarse_links",
    )(face_y, face_z, *prepared)


def place_call(site_map, codes, order):
    return pl.pallas_call(
        lambda *refs: place_kernel(order, *refs),
        in_specs=[pl.BlockSpec(memory_space=pltpu.SMEM), pl.BlockSpec(memory_space=pltpu.VMEM)],
        out_specs=pl.BlockSpec(memory_space=pl.ANY),
        out_shape=jax.ShapeDtypeStruct((COUNT, 144, 128), F32),
        scratch_shapes=[
            pltpu.VMEM((COUNT, 144, 128), F32),
            pltpu.SMEM((COUNT,), jnp.int32),
            pltpu.SemaphoreType.DMA((COUNT // CHUNK,)),
        ],
        compiler_params=pltpu.CompilerParams(vmem_limit_bytes=40 * 2**20),
        name="place_links",
    )(site_map, codes)


def passed_back(value, axis):
    count = lax.axis_size(axis)
    return lax.ppermute(value, axis, [(source, (source - 1) % count) for source in range(count)])


def flat_index(z, core):
    return (z % 4) * 8 + (z // 4) * 2 + core


def gathered(code):
    pairs = [[flat_index(z, core), flat_index(z + 1, core)] for z in range(0, 16, 2) for core in range(2)]
    rings = [[flat_index(z + odd, core) for z in range(0, 16, 2) for core in range(2)] for odd in range(2)]
    names = ("gx", "gy")
    code = lax.all_gather(code[None], names, axis=0, tiled=True, axis_index_groups=pairs)
    code = lax.all_gather(code, names, axis=0, tiled=True, axis_index_groups=rings)
    return code, [index for pair in pairs for index in pair]


def body(near_null, gauge, site_map):
    own, start, mix, face_y, face_x, face_z = first_call(near_null.reshape(2 * SITES, FULL))
    face_y = passed_back(face_y, "gy")
    face_x = passed_back(face_x, "gx")
    face_z = passed_back(face_z, "zt")
    prepared = own_call(face_x, own, start, mix, gauge.reshape(2 * SITES, LINKS))
    code = second_call(face_y, face_z, prepared)
    codes, order = gathered(code)
    placed = place_call(site_map, codes, order)
    placed = placed.reshape(COUNT, 72, 2, 128).transpose(0, 2, 1, 3)
    return placed.reshape(1, COUNT, 2, 9216)


def solution(mesh):
    return jax.shard_map(
        body,
        mesh=mesh,
        in_specs=(P("gx", "gy", "zt", None, None), P("gx", "gy", "zt", None, None), P("zt", None)),
        out_specs=P("zt", None, None, None),
        check_vma=False,
    )
```

```python
import jax
import jax.numpy as jnp
import numpy as np
from jax import lax
from jax.experimental import pallas as pl
from jax.experimental.pallas import tpu as pltpu
from jax.sharding import PartitionSpec as P

F32 = jnp.float32
BF16 = jnp.bfloat16
SITES = 64
FACE = 16
NVEC = 24
GROUPS = 12
WIDE = GROUPS * NVEC
PAD = 384
FULL = 4 * WIDE
LINKS = 144
COUNT = 32
CHUNK = 4
MIX_ROW = 288
SENT = 336
ARRIVALS = ("x", "z near", "y early", "z far", "y late")
TARGET = 64.0
GAMMA = [
    ((0, 1, -1j), (1, 0, -1j)),
    ((0, 1, -1), (1, 0, 1)),
    ((0, 0, -1j), (1, 1, 1j)),
    ((0, 0, 1), (1, 1, 1)),
]


def dot(left, right, dims=((1,), (0,))):
    return lax.dot_general(left, right, (dims, ((), ())), preferred_element_type=F32)


def bf16_parts(value, count):
    parts = []
    for _ in range(count):
        part = value.astype(BF16)
        parts.append(part)
        value = value - part.astype(F32)
    return parts


def dot_parts(parts, ones):
    rows = parts[0].shape[0]
    out = dot(jnp.concatenate(parts, axis=0), ones)
    total = out[(len(parts) - 1) * rows :]
    for index in reversed(range(len(parts) - 1)):
        total = total + out[index * rows : (index + 1) * rows]
    return total


def time_rows(block):
    return jnp.concatenate([block[:, step * WIDE : (step + 1) * WIDE] for step in range(4)], axis=0)


def lane_of(shape):
    return lax.broadcasted_iota(jnp.int32, shape, 1)


def row_of(shape):
    return lax.broadcasted_iota(jnp.int32, shape, 0)


def ones_where(condition, dtype):
    return jnp.where(condition, 1.0, 0.0).astype(dtype)


def all_rows():
    shape = (SITES, 2 * SITES)
    first = lane_of(shape) - 2 * row_of(shape)
    return [ones_where(first == part, BF16) for part in range(2)]


def layer_rows(layer):
    shape = (FACE, 2 * SITES)
    lanes, rows = lane_of(shape), row_of(shape)
    sites = [layer * 16 + rows, (rows // 4) * 16 + layer * 4 + rows % 4, rows * 4 + layer]
    return [ones_where(lanes == 2 * site + part, BF16) for site in sites for part in range(2)]


def gram_fold():
    shape = (WIDE, 128)
    rows = row_of(shape)
    away = lane_of(shape) - ((rows // 144) * 48 + rows % NVEC)
    return jnp.concatenate([ones_where(away == part * NVEC, BF16) for part in range(2)], axis=1)


def mixing_spread():
    shape = (128, PAD)
    lanes, rows = lane_of(shape), row_of(shape)
    blocks = []
    for part in range(2):
        for chirality in range(2):
            inside = (lanes >= chirality * 144) & (lanes < chirality * 144 + 144)
            source = jnp.where(inside, lanes % NVEC + chirality * 48 + part * NVEC, -1)
            blocks.append(ones_where(rows == source, BF16))
    return jnp.concatenate(blocks, axis=1)


def colour_turns():
    shape = (WIDE, PAD)
    lanes, rows = lane_of(shape), row_of(shape)
    colour = (lanes // NVEC) % 3
    blocks = []
    for turn in (1, 2):
        source = lanes + NVEC * jnp.where(colour + turn >= 3, turn - 3, turn)
        blocks.append(ones_where((rows == source) & (lanes < WIDE), BF16))
    return jnp.concatenate(blocks, axis=1)


def link_spread():
    shape = (16, PAD)
    lanes, rows = lane_of(shape), row_of(shape)
    colour = (lanes // NVEC) % 3
    blocks = []
    for turn in range(3):
        source = colour * 3 + (colour + turn) % 3
        blocks.append(ones_where((rows == source) & (lanes < WIDE), BF16))
    return jnp.concatenate(blocks, axis=1)


def link_pick():
    shape = (LINKS, 128)
    lanes = lane_of(shape)
    start = jnp.where(lanes < 9, row_of(shape) - lanes, -1)
    starts = [9 * piece for piece in range(12)] + [135]
    return jnp.concatenate([ones_where(start == first, BF16) for first in starts], axis=1)


def mixing_rows(hermitian, hermitian_turned):
    shape = (8, 128)
    lanes, rows = lane_of(shape), row_of(shape)
    lower = lanes < 48
    blocks = range(3)

    def split(value):
        return [value[8 * block : 8 * block + 8] for block in blocks]

    gram, gram_turned = split(hermitian), split(hermitian_turned)
    mix = [jnp.where((lanes % 48 == rows + 8 * block) & (lanes < 96), 1.0, 0.0) for block in blocks]
    turned = [jnp.where((lanes % 48 == rows + 8 * block + 24) & (lanes < 96), 1.0, 0.0) for block in blocks]
    weights = []

    def spread(value, at):
        return jnp.where(lower, value[:, at : at + 1], value[:, 48 + at : 49 + at])

    for column in range(NVEC):
        own, place = column // 8, column % 8
        here = slice(place, place + 1)
        row, row_turned = gram[own][here], gram_turned[own][here]
        mix_row, mix_turned = mix[own][here], turned[own][here]
        product = row * mix_row
        both = jnp.concatenate([jnp.where(lower[:1], product, 0.0), jnp.where(lower[:1], 0.0, product)], axis=0)
        both = jnp.sum(both, axis=1, keepdims=True)
        weight = jnp.where(lower[:1], both[:1], both[1:])
        weights.append(weight)
        active = [block for block in blocks if 8 * block + 7 > column]
        if not active:
            break
        ratio = TARGET / weight
        for block in active:
            a_re, a_im = spread(gram[block], column), spread(gram[block], column + 24)
            scale = jnp.where(rows + 8 * block > column, ratio, 0.0) if block == own else ratio
            gram_step = a_re * row + a_im * row_turned
            gram_turned_step = a_re * row_turned - a_im * row
            mix_step = a_re * mix_row + a_im * mix_turned
            turned_step = a_re * mix_turned - a_im * mix_row
            gram[block] = gram[block] - scale * gram_step
            gram_turned[block] = gram_turned[block] - scale * gram_turned_step
            mix[block] = mix[block] - scale * mix_step
            turned[block] = turned[block] - scale * turned_step
    weights = jnp.concatenate(weights, axis=0)
    return jnp.concatenate(mix, axis=0) * jnp.sqrt(TARGET / weights)


def first_kernel(nn_ref, own_ref, start_ref, mix_ref, *sent_refs):
    selection = jnp.concatenate(all_rows() + layer_rows(3) + layer_rows(0), axis=0)
    chosen = dot(selection, nn_ref[...]).astype(BF16)
    every = chosen[:128]
    tall = time_rows(every)
    tall_turned = time_rows(jnp.concatenate([every[64:], -every[:64]], axis=0))
    wide_re = dot(tall, tall, ((0,), (0,)))
    wide_im = dot(tall, tall_turned, ((0,), (0,)))
    group = lane_of((NVEC, WIDE)) // NVEC
    fold_re = jnp.zeros((NVEC, WIDE), F32)
    fold_im = jnp.zeros((NVEC, WIDE), F32)
    for index in range(GROUPS):
        here = slice(index * NVEC, (index + 1) * NVEC)
        fold_re = jnp.where(group == index, wide_re[here], fold_re)
        fold_im = jnp.where(group == index, wide_im[here], fold_im)
    folded = dot_parts(bf16_parts(jnp.concatenate([fold_re, fold_im], axis=0), 3), gram_fold())
    hermitian = folded[:NVEC, :128] - folded[NVEC:, 128:]
    hermitian_turned = folded[NVEC:, :128] + folded[:NVEC, 128:]
    mix = mixing_rows(hermitian, hermitian_turned)
    mix_ref[...] = mix
    packed = jnp.concatenate(bf16_parts(mix, 2), axis=0)
    for name, out in zip(ARRIVALS, sent_refs):
        first = 224 + 32 * "xyz".index(name[0])
        for column in range(9):
            out[column * 32 : column * 32 + 32, :] = chosen[first : first + 32, column * 128 : (column + 1) * 128]
        out[MIX_ROW:, :] = packed
    for axis in range(3):
        first = 128 + 32 * axis
        own_ref[axis, :64] = time_rows(chosen[first : first + 16])
        own_ref[axis, 64:] = time_rows(chosen[first + 16 : first + 32])
    own_ref[3] = every[:, 3 * WIDE :]
    start_ref[...] = every[:, :WIDE]


def hop(gauge, same, turned, sign):
    moved_re = jnp.zeros((64, WIDE), F32)
    moved_im = jnp.zeros((64, WIDE), F32)
    for turn in range(3):
        u = gauge[:, turn * PAD : turn * PAD + WIDE].astype(F32)
        v = same.astype(F32) if turn == 0 else turned[:, (turn - 1) * PAD : (turn - 1) * PAD + WIDE]
        moved_re = moved_re + (u[:64] * v[:64] - u[64:] * v[64:])
        moved_im = moved_im + (u[:64] * v[64:] + u[64:] * v[:64])
    if sign < 0:
        moved_re, moved_im = -moved_re, -moved_im
    top_re, top_im = moved_re.astype(BF16), moved_im.astype(BF16)
    low_re = (moved_re - top_re.astype(F32)).astype(BF16)
    low_im = (moved_im - top_im.astype(F32)).astype(BF16)
    return (
        jnp.concatenate([top_re, top_im, low_re, low_im], axis=0),
        jnp.concatenate([top_im, -top_re, low_im, -low_re], axis=0),
    )


def spin_fold(wide_re, wide_im, direction):
    group = lane_of((NVEC, WIDE)) // NVEC
    fold_re, fold_im = [], []
    for chirality in range(2):
        sum_re = jnp.zeros((NVEC, WIDE), F32)
        sum_im = jnp.zeros((NVEC, WIDE), F32)
        for row_spin, col_spin, value in GAMMA[direction]:
            if chirality == 1:
                row_spin, col_spin, value = col_spin, row_spin, np.conj(value)
            factor = -value
            for colour in range(3):
                index = chirality * 6 + row_spin * 3 + colour
                here = slice(index * NVEC, (index + 1) * NVEC)
                at_re, at_im = wide_re[here], wide_im[here]
                if np.imag(factor) != 0:
                    over_re, over_im = -float(np.imag(factor)) * at_im, float(np.imag(factor)) * at_re
                else:
                    over_re, over_im = float(np.real(factor)) * at_re, float(np.real(factor)) * at_im
                partner = (1 - chirality) * 6 + col_spin * 3 + colour
                sum_re = jnp.where(group == index, at_re, jnp.where(group == partner, over_re, sum_re))
                sum_im = jnp.where(group == index, at_im, jnp.where(group == partner, over_im, sum_im))
        fold_re.append(sum_re)
        fold_im.append(sum_im)
    return jnp.concatenate(fold_re + fold_im, axis=0)


def spread_mixing(parts, ones):
    rows = parts[0].shape[0]
    out = dot(jnp.concatenate(parts, axis=0), ones).astype(BF16)
    gap = jnp.zeros((80, WIDE), BF16)
    result = []
    for first in range(0, rows, NVEC):
        pair = []
        for index in range(2):
            here = slice(index * rows + first, index * rows + first + NVEC)
            blocks = [out[here, block * PAD : block * PAD + WIDE] for block in range(4)]
            pair.append(jnp.concatenate([blocks[0], blocks[1], gap, blocks[2], blocks[3]], axis=0))
        result.append(pair)
    return result


def link_matrix(folded, mixing, left):
    top, low = bf16_parts(folded, 2)
    by = dot(jnp.concatenate([top, low], axis=0), mixing[0], ((1,), (1,)))
    by = by[:96] + (by[96:] + dot(top, mixing[1], ((1,), (1,))))
    by_re, by_im = by[:, :48], by[:, 128:]
    half = jnp.concatenate([by_re[:48] - by_im[48:], jnp.zeros((48, 80), F32), by_im[:48] + by_re[48:]], axis=1)
    top, low = bf16_parts(half, 2)
    on = dot(left, top)
    on = on[:96] + (on[96:] + dot(left[:96], low))
    return on[:48, :48] + on[48:, 128:], on[:48, 128:] - on[48:, :48]


def next_face(*refs):
    value = refs[0][...].astype(F32)
    if len(refs) == 2:
        value = value + refs[1][...].astype(F32)
    packed = value.astype(BF16)
    face = jnp.concatenate([packed[column * 32 : column * 32 + 32] for column in range(9)], axis=1)
    parts = value[MIX_ROW:]
    parts = [parts[:NVEC].astype(BF16), parts[NVEC:].astype(BF16)]
    return jnp.concatenate([time_rows(face[:16]), time_rows(face[16:])], axis=0), parts


def write_rows(links, flat_ref, order_ref):
    count = 12 * len(links)
    for index, (_, matrix_re, matrix_im) in enumerate(links):
        flat_ref[index * 96 : index * 96 + 48, :] = matrix_re
        flat_ref[index * 96 + 48 : index * 96 + 96, :] = matrix_im
    long = jnp.concatenate([flat_ref[pl.ds(row, count, stride=8), :] for row in range(8)], axis=1)
    for index, (direction, _, _) in enumerate(links):
        for part in range(2):
            first = (index * 2 + part) * 6
            for third in range(3):
                target = direction * 36 + third * 2 + part
                order_ref[pl.ds(target, 6, stride=6), :] = long[first : first + 6, third * 128 : (third + 1) * 128]


def prepare_kernel(
    own_ref, mix_ref, ga_ref, far_ref, late_ref,
    gauge_ref, turns_ref, spread_ref, rows_ref, left_ref, far_out_ref, late_out_ref,
):
    far_out_ref[...] = far_ref[...]
    late_out_ref[...] = late_ref[...]
    selection = jnp.concatenate(all_rows() + layer_rows(3), axis=0)
    face_links = dot(selection, ga_ref[...]).astype(BF16)
    picked = dot(face_links, link_pick()).astype(BF16)
    link_rows = []
    for axis in range(3):
        first = 128 + 32 * axis
        for part in range(2):
            for step in range(4):
                piece = axis * 4 + step
                link_rows.append(picked[first + 16 * part : first + 16 * part + 16, piece * 128 : piece * 128 + 16])
    link_rows.append(picked[:128, 12 * 128 : 12 * 128 + 16])
    gauge = dot(jnp.concatenate(link_rows, axis=0), link_spread()).astype(BF16)
    gauge_ref[...] = gauge
    turns_ref[...] = colour_turns()
    spread_ref[...] = mixing_spread()
    mix = mix_ref[...]
    zero = jnp.zeros((NVEC, NVEC), F32)
    left = []
    for part in range(2):
        first = mix[:, part * 24 : part * 24 + 24]
        second = mix[:, 48 + part * 24 : 72 + part * 24]
        left += [jnp.concatenate([first, zero], axis=1), jnp.concatenate([zero, second], axis=1)]
    left = jnp.concatenate(bf16_parts(jnp.concatenate(left, axis=0), 2), axis=0)
    left_ref[...] = left
    for axis in range(4):
        mine = own_ref[axis]
        rows_ref[axis] = jnp.concatenate([mine, mine], axis=0).T


def own_kernel(rx_ref, start_ref, mix_ref, gauge_ref, turns_ref, spread_ref, rows_ref, left_ref, order_ref, flat_ref):
    mix = mix_ref[...]
    left = left_ref[...]
    face, mix_x = next_face(rx_ref)
    ahead = jnp.concatenate([face, start_ref[...]], axis=0)
    turned = dot(ahead, turns_ref[...])
    mixings = spread_mixing([jnp.concatenate(pair, axis=0) for pair in zip(mix_x, bf16_parts(mix, 2))], spread_ref[...])
    links = []
    for index, direction in enumerate((0, 3)):
        here = slice(index * 128, index * 128 + 128)
        to_re, to_im = hop(gauge_ref[direction * 128 : direction * 128 + 128, :], ahead[here], turned[here], 1.0 - 2.0 * index)
        folded = spin_fold(dot(rows_ref[direction], to_re), dot(rows_ref[direction], to_im), direction)
        links.append((direction, *link_matrix(folded, mixings[index], left)))
    order_ref[...] = jnp.zeros((144, 128), F32)
    write_rows(links, flat_ref, order_ref)


def second_kernel(
    near_ref, early_ref, far_ref, late_ref, gauge_ref, turns_ref, spread_ref, rows_ref, left_ref, start_ref,
    code_ref, flat_ref, order_ref,
):
    order_ref[...] = start_ref[...]
    left = left_ref[...]
    face_y, mix_y = next_face(early_ref, late_ref)
    face_z, mix_z = next_face(near_ref, far_ref)
    ahead = jnp.concatenate([face_y, face_z], axis=0)
    turned = dot(ahead, turns_ref[...])
    mixings = spread_mixing([jnp.concatenate(pair, axis=0) for pair in zip(mix_y, mix_z)], spread_ref[...])
    links = []
    for index, direction in enumerate((1, 2)):
        here = slice(index * 128, index * 128 + 128)
        to_re, to_im = hop(gauge_ref[direction * 128 : direction * 128 + 128, :], ahead[here], turned[here], 1.0)
        rows = rows_ref[direction]
        folded = spin_fold(dot(rows, to_re), dot(rows, to_im), direction)
        links.append((direction, *link_matrix(folded, mixings[index], left)))
    write_rows(links, flat_ref, order_ref)
    powers = []
    for block in range(9):
        values = order_ref[block * 16 : block * 16 + 16, :]
        largest = jnp.max(jnp.abs(values), axis=0, keepdims=True)
        power = jnp.clip(jnp.ceil(jnp.log2(jnp.maximum(largest, 1e-30)) + 1e-3), -100.0, 120.0)
        scaled = values * jnp.exp2(-power) * 32767.0
        scaled = jnp.clip(jnp.round(scaled), -32767.0, 32767.0)
        code_ref[block * 16 : block * 16 + 16, :] = scaled.astype(jnp.int32).astype(jnp.int16)
        powers.append(power)
    powers = jnp.concatenate(powers + [jnp.zeros((7, 128), F32)], axis=0)
    code_ref[144:160, :] = powers.astype(jnp.int32).astype(jnp.int16)


def place_kernel(order, site_ref, code_ref, out_ref, wide_ref, source_ref, sem_ref):
    for index in range(COUNT):
        source_ref[site_ref[0, order[index]]] = index
    copies = []
    for site in range(COUNT):
        source = source_ref[site]
        power = code_ref[source, 144:160, :].astype(jnp.int32).astype(F32)
        scale = jnp.exp2(power) * (1.0 / 32767.0)
        for block in range(9):
            values = code_ref[source, block * 16 : block * 16 + 16, :].astype(jnp.int32).astype(F32)
            wide_ref[site, block * 16 : block * 16 + 16, :] = values * scale[block : block + 1]
        if site % CHUNK == CHUNK - 1:
            here = pl.ds(site - CHUNK + 1, CHUNK)
            copy = pltpu.make_async_copy(wide_ref.at[here], out_ref.at[here], sem_ref.at[site // CHUNK])
            copy.start()
            copies.append(copy)
    for copy in copies:
        copy.wait()


def first_call(block):
    return pl.pallas_call(
        first_kernel,
        out_shape=[
            jax.ShapeDtypeStruct((4, 128, WIDE), BF16),
            jax.ShapeDtypeStruct((128, WIDE), BF16),
            jax.ShapeDtypeStruct((NVEC, 128), F32),
        ]
        + [jax.ShapeDtypeStruct((SENT, 128), BF16)] * len(ARRIVALS),
        compiler_params=pltpu.CompilerParams(vmem_limit_bytes=40 * 2**20),
        name="gram_and_mixing",
    )(block)


def prepare_call(own, mix, gauge, far, late):
    return pl.pallas_call(
        prepare_kernel,
        out_shape=[
            jax.ShapeDtypeStruct((512, 3 * PAD), BF16),
            jax.ShapeDtypeStruct((WIDE, 2 * PAD), BF16),
            jax.ShapeDtypeStruct((128, 4 * PAD), BF16),
            jax.ShapeDtypeStruct((4, WIDE, 256), BF16),
            jax.ShapeDtypeStruct((192, 48), BF16),
            jax.ShapeDtypeStruct((SENT, 128), BF16),
            jax.ShapeDtypeStruct((SENT, 128), BF16),
        ],
        compiler_params=pltpu.CompilerParams(vmem_limit_bytes=40 * 2**20),
        cost_estimate=pl.CostEstimate(flops=10**9, bytes_accessed=4 * 10**6, transcendentals=0),
        name="prepare",
    )(own, mix, gauge, far, late)


def own_call(face_x, start, mix, prepared):
    return pl.pallas_call(
        own_kernel,
        out_shape=jax.ShapeDtypeStruct((144, 128), F32),
        scratch_shapes=[pltpu.VMEM((192, 48), F32)],
        compiler_params=pltpu.CompilerParams(vmem_limit_bytes=40 * 2**20),
        cost_estimate=pl.CostEstimate(flops=10**9, bytes_accessed=4 * 10**6, transcendentals=0),
        name="own_part",
    )(face_x, start, mix, *prepared)


def second_call(faces, prepared):
    return pl.pallas_call(
        second_kernel,
        out_shape=jax.ShapeDtypeStruct((160, 128), jnp.int16),
        scratch_shapes=[pltpu.VMEM((192, 48), F32), pltpu.VMEM((144, 128), F32)],
        compiler_params=pltpu.CompilerParams(vmem_limit_bytes=40 * 2**20),
        name="coarse_links",
    )(*faces, *prepared)


def place_call(site_map, codes, order):
    return pl.pallas_call(
        lambda *refs: place_kernel(order, *refs),
        in_specs=[pl.BlockSpec(memory_space=pltpu.SMEM), pl.BlockSpec(memory_space=pltpu.VMEM)],
        out_specs=pl.BlockSpec(memory_space=pl.ANY),
        out_shape=jax.ShapeDtypeStruct((COUNT, 144, 128), F32),
        scratch_shapes=[
            pltpu.VMEM((COUNT, 144, 128), F32),
            pltpu.SMEM((COUNT,), jnp.int32),
            pltpu.SemaphoreType.DMA((COUNT // CHUNK,)),
        ],
        compiler_params=pltpu.CompilerParams(vmem_limit_bytes=40 * 2**20),
        name="place_links",
    )(site_map, codes)


def passed_back(value, name):
    axis = {"x": "gx", "y": "gy", "z": "zt"}[name[0]]
    if axis == "gy":
        columns = [column for column in range(16) if (column % 4 == 0) == name.endswith("early")]
        pairs = [(source * 16 + column, (source - 1) % 8 * 16 + column) for source in range(8) for column in columns]
        return lax.ppermute(value, ("gy", "zt"), pairs)
    count = lax.axis_size(axis)
    sources = [source for source in range(count) if axis == "gx" or (source % 4 == 0) == name.endswith("far")]
    return lax.ppermute(value, axis, [(source, (source - 1) % count) for source in sources])


def flat_index(z, core):
    return (z % 4) * 8 + (z // 4) * 2 + core


def gathered(code):
    pairs = [[flat_index(z, core), flat_index(z + 1, core)] for z in range(0, 16, 2) for core in range(2)]
    rings = [[flat_index(z + odd, core) for z in range(0, 16, 2) for core in range(2)] for odd in range(2)]
    names = ("gx", "gy")
    code = lax.all_gather(code[None], names, axis=0, tiled=True, axis_index_groups=pairs)
    code = lax.all_gather(code, names, axis=0, tiled=True, axis_index_groups=rings)
    return code, [index for pair in pairs for index in pair]


def body(near_null, gauge, site_map):
    own, start, mix, *faces = first_call(near_null.reshape(2 * SITES, FULL))
    faces = dict(zip(ARRIVALS, faces))
    *prepared, faces["z far"], faces["y late"] = prepare_call(
        own, mix, gauge.reshape(2 * SITES, LINKS), faces["z far"], faces["y late"]
    )
    face_x, *faces = [passed_back(faces[name], name) for name in ARRIVALS]
    code = second_call(faces, [*prepared, own_call(face_x, start, mix, prepared)])
    codes, order = gathered(code)
    placed = place_call(site_map, codes, order)
    placed = placed.reshape(COUNT, 72, 2, 128).transpose(0, 2, 1, 3)
    return placed.reshape(1, COUNT, 2, 9216)


def solution(mesh):
    return jax.shard_map(
        body,
        mesh=mesh,
        in_specs=(P("gx", "gy", "zt", None, None), P("gx", "gy", "zt", None, None), P("zt", None)),
        out_specs=P("zt", None, None, None),
        check_vma=False,
    )
```

```python
import jax
import jax.numpy as jnp
import numpy as np
from jax import lax
from jax.experimental import pallas as pl
from jax.experimental.pallas import tpu as pltpu
from jax.sharding import PartitionSpec as P

F32 = jnp.float32
BF16 = jnp.bfloat16
SITES = 64
FACE = 16
NVEC = 24
GROUPS = 12
WIDE = GROUPS * NVEC
PAD = 384
FULL = 4 * WIDE
LINKS = 144
COUNT = 32
CHUNK = 4
MIX_ROW = 288
SENT = 336
TARGET = 64.0
GAMMA = [
    ((0, 1, -1j), (1, 0, -1j)),
    ((0, 1, -1), (1, 0, 1)),
    ((0, 0, -1j), (1, 1, 1j)),
    ((0, 0, 1), (1, 1, 1)),
]


def dot(left, right, dims=((1,), (0,))):
    return lax.dot_general(left, right, (dims, ((), ())), preferred_element_type=F32)


def bf16_parts(value, count):
    parts = []
    for _ in range(count):
        part = value.astype(BF16)
        parts.append(part)
        value = value - part.astype(F32)
    return parts


def dot_parts(parts, ones):
    rows = parts[0].shape[0]
    out = dot(jnp.concatenate(parts, axis=0), ones)
    total = out[(len(parts) - 1) * rows :]
    for index in reversed(range(len(parts) - 1)):
        total = total + out[index * rows : (index + 1) * rows]
    return total


def time_rows(block):
    return jnp.concatenate([block[:, step * WIDE : (step + 1) * WIDE] for step in range(4)], axis=0)


def lane_of(shape):
    return lax.broadcasted_iota(jnp.int32, shape, 1)


def row_of(shape):
    return lax.broadcasted_iota(jnp.int32, shape, 0)


def ones_where(condition, dtype):
    return jnp.where(condition, 1.0, 0.0).astype(dtype)


def all_rows():
    shape = (SITES, 2 * SITES)
    first = lane_of(shape) - 2 * row_of(shape)
    return [ones_where(first == part, BF16) for part in range(2)]


def layer_rows(layer):
    shape = (FACE, 2 * SITES)
    lanes, rows = lane_of(shape), row_of(shape)
    sites = [layer * 16 + rows, (rows // 4) * 16 + layer * 4 + rows % 4, rows * 4 + layer]
    return [ones_where(lanes == 2 * site + part, BF16) for site in sites for part in range(2)]


def gram_fold():
    shape = (WIDE, 128)
    rows = row_of(shape)
    away = lane_of(shape) - ((rows // 144) * 48 + rows % NVEC)
    return jnp.concatenate([ones_where(away == part * NVEC, BF16) for part in range(2)], axis=1)


def mixing_spread():
    shape = (128, PAD)
    lanes, rows = lane_of(shape), row_of(shape)
    blocks = []
    for part in range(2):
        for chirality in range(2):
            inside = (lanes >= chirality * 144) & (lanes < chirality * 144 + 144)
            source = jnp.where(inside, lanes % NVEC + chirality * 48 + part * NVEC, -1)
            blocks.append(ones_where(rows == source, BF16))
    return jnp.concatenate(blocks, axis=1)


def colour_turns():
    shape = (WIDE, PAD)
    lanes, rows = lane_of(shape), row_of(shape)
    colour = (lanes // NVEC) % 3
    blocks = []
    for turn in (1, 2):
        source = lanes + NVEC * jnp.where(colour + turn >= 3, turn - 3, turn)
        blocks.append(ones_where((rows == source) & (lanes < WIDE), BF16))
    return jnp.concatenate(blocks, axis=1)


def link_spread():
    shape = (16, PAD)
    lanes, rows = lane_of(shape), row_of(shape)
    colour = (lanes // NVEC) % 3
    blocks = []
    for turn in range(3):
        source = colour * 3 + (colour + turn) % 3
        blocks.append(ones_where((rows == source) & (lanes < WIDE), BF16))
    return jnp.concatenate(blocks, axis=1)


def link_pick():
    shape = (LINKS, 128)
    lanes = lane_of(shape)
    start = jnp.where(lanes < 9, row_of(shape) - lanes, -1)
    starts = [9 * piece for piece in range(12)] + [135]
    return jnp.concatenate([ones_where(start == first, BF16) for first in starts], axis=1)


def mixing_rows(hermitian, hermitian_turned):
    shape = (8, 128)
    lanes, rows = lane_of(shape), row_of(shape)
    lower = lanes < 48
    blocks = range(3)

    def split(value):
        return [value[8 * block : 8 * block + 8] for block in blocks]

    gram, gram_turned = split(hermitian), split(hermitian_turned)
    mix = [jnp.where((lanes % 48 == rows + 8 * block) & (lanes < 96), 1.0, 0.0) for block in blocks]
    turned = [jnp.where((lanes % 48 == rows + 8 * block + 24) & (lanes < 96), 1.0, 0.0) for block in blocks]
    weights = []

    def spread(value, at):
        return jnp.where(lower, value[:, at : at + 1], value[:, 48 + at : 49 + at])

    for column in range(NVEC):
        own, place = column // 8, column % 8
        here = slice(place, place + 1)
        row, row_turned = gram[own][here], gram_turned[own][here]
        mix_row, mix_turned = mix[own][here], turned[own][here]
        product = row * mix_row
        both = jnp.concatenate([jnp.where(lower[:1], product, 0.0), jnp.where(lower[:1], 0.0, product)], axis=0)
        both = jnp.sum(both, axis=1, keepdims=True)
        weight = jnp.where(lower[:1], both[:1], both[1:])
        weights.append(weight)
        active = [block for block in blocks if 8 * block + 7 > column]
        if not active:
            break
        ratio = TARGET / weight
        for block in active:
            a_re, a_im = spread(gram[block], column), spread(gram[block], column + 24)
            scale = jnp.where(rows + 8 * block > column, ratio, 0.0) if block == own else ratio
            gram_step = a_re * row + a_im * row_turned
            gram_turned_step = a_re * row_turned - a_im * row
            mix_step = a_re * mix_row + a_im * mix_turned
            turned_step = a_re * mix_turned - a_im * mix_row
            gram[block] = gram[block] - scale * gram_step
            gram_turned[block] = gram_turned[block] - scale * gram_turned_step
            mix[block] = mix[block] - scale * mix_step
            turned[block] = turned[block] - scale * turned_step
    weights = jnp.concatenate(weights, axis=0)
    return jnp.concatenate(mix, axis=0) * jnp.sqrt(TARGET / weights)


def first_kernel(nn_ref, own_ref, start_ref, mix_ref, py_ref, px_ref, pz_ref):
    selection = jnp.concatenate(all_rows() + layer_rows(3) + layer_rows(0), axis=0)
    chosen = dot(selection, nn_ref[...]).astype(BF16)
    every = chosen[:128]
    tall = time_rows(every)
    tall_turned = time_rows(jnp.concatenate([every[64:], -every[:64]], axis=0))
    wide_re = dot(tall, tall, ((0,), (0,)))
    wide_im = dot(tall, tall_turned, ((0,), (0,)))
    group = lane_of((NVEC, WIDE)) // NVEC
    fold_re = jnp.zeros((NVEC, WIDE), F32)
    fold_im = jnp.zeros((NVEC, WIDE), F32)
    for index in range(GROUPS):
        here = slice(index * NVEC, (index + 1) * NVEC)
        fold_re = jnp.where(group == index, wide_re[here], fold_re)
        fold_im = jnp.where(group == index, wide_im[here], fold_im)
    folded = dot_parts(bf16_parts(jnp.concatenate([fold_re, fold_im], axis=0), 3), gram_fold())
    hermitian = folded[:NVEC, :128] - folded[NVEC:, 128:]
    hermitian_turned = folded[NVEC:, :128] + folded[:NVEC, 128:]
    mix = mixing_rows(hermitian, hermitian_turned)
    mix_ref[...] = mix
    packed = jnp.concatenate(bf16_parts(mix, 2), axis=0)
    for axis, out in enumerate((px_ref, py_ref, pz_ref)):
        first = 224 + 32 * axis
        for column in range(9):
            out[column * 32 : column * 32 + 32, :] = chosen[first : first + 32, column * 128 : (column + 1) * 128]
        out[MIX_ROW:, :] = packed
    for axis in range(3):
        first = 128 + 32 * axis
        own_ref[axis, :64] = time_rows(chosen[first : first + 16])
        own_ref[axis, 64:] = time_rows(chosen[first + 16 : first + 32])
    own_ref[3] = every[:, 3 * WIDE :]
    start_ref[...] = every[:, :WIDE]


def hop(gauge, same, turned, sign):
    moved_re = jnp.zeros((64, WIDE), F32)
    moved_im = jnp.zeros((64, WIDE), F32)
    for turn in range(3):
        u = gauge[:, turn * PAD : turn * PAD + WIDE].astype(F32)
        v = same.astype(F32) if turn == 0 else turned[:, (turn - 1) * PAD : (turn - 1) * PAD + WIDE]
        moved_re = moved_re + (u[:64] * v[:64] - u[64:] * v[64:])
        moved_im = moved_im + (u[:64] * v[64:] + u[64:] * v[:64])
    if sign < 0:
        moved_re, moved_im = -moved_re, -moved_im
    top_re, top_im = moved_re.astype(BF16), moved_im.astype(BF16)
    low_re = (moved_re - top_re.astype(F32)).astype(BF16)
    low_im = (moved_im - top_im.astype(F32)).astype(BF16)
    return (
        jnp.concatenate([top_re, top_im, low_re, low_im], axis=0),
        jnp.concatenate([top_im, -top_re, low_im, -low_re], axis=0),
    )


def spin_fold(wide_re, wide_im, direction):
    group = lane_of((NVEC, WIDE)) // NVEC
    fold_re, fold_im = [], []
    for chirality in range(2):
        sum_re = jnp.zeros((NVEC, WIDE), F32)
        sum_im = jnp.zeros((NVEC, WIDE), F32)
        for row_spin, col_spin, value in GAMMA[direction]:
            if chirality == 1:
                row_spin, col_spin, value = col_spin, row_spin, np.conj(value)
            factor = -value
            for colour in range(3):
                index = chirality * 6 + row_spin * 3 + colour
                here = slice(index * NVEC, (index + 1) * NVEC)
                at_re, at_im = wide_re[here], wide_im[here]
                if np.imag(factor) != 0:
                    over_re, over_im = -float(np.imag(factor)) * at_im, float(np.imag(factor)) * at_re
                else:
                    over_re, over_im = float(np.real(factor)) * at_re, float(np.real(factor)) * at_im
                partner = (1 - chirality) * 6 + col_spin * 3 + colour
                sum_re = jnp.where(group == index, at_re, jnp.where(group == partner, over_re, sum_re))
                sum_im = jnp.where(group == index, at_im, jnp.where(group == partner, over_im, sum_im))
        fold_re.append(sum_re)
        fold_im.append(sum_im)
    return jnp.concatenate(fold_re + fold_im, axis=0)


def spread_mixing(parts, ones):
    rows = parts[0].shape[0]
    out = dot(jnp.concatenate(parts, axis=0), ones).astype(BF16)
    gap = jnp.zeros((80, WIDE), BF16)
    result = []
    for first in range(0, rows, NVEC):
        pair = []
        for index in range(2):
            here = slice(index * rows + first, index * rows + first + NVEC)
            blocks = [out[here, block * PAD : block * PAD + WIDE] for block in range(4)]
            pair.append(jnp.concatenate([blocks[0], blocks[1], gap, blocks[2], blocks[3]], axis=0))
        result.append(pair)
    return result


def link_matrix(folded, mixing, left):
    top, low = bf16_parts(folded, 2)
    by = dot(jnp.concatenate([top, low], axis=0), mixing[0], ((1,), (1,)))
    by = by[:96] + (by[96:] + dot(top, mixing[1], ((1,), (1,))))
    by_re, by_im = by[:, :48], by[:, 128:]
    half = jnp.concatenate([by_re[:48] - by_im[48:], jnp.zeros((48, 80), F32), by_im[:48] + by_re[48:]], axis=1)
    top, low = bf16_parts(half, 2)
    on = dot(left, top)
    on = on[:96] + (on[96:] + dot(left[:96], low))
    return on[:48, :48] + on[48:, 128:], on[:48, 128:] - on[48:, :48]


def next_face(ref):
    face = jnp.concatenate([ref[column * 32 : column * 32 + 32, :] for column in range(9)], axis=1)
    parts = ref[MIX_ROW:SENT, :].astype(F32)
    parts = [parts[:NVEC].astype(BF16), parts[NVEC:].astype(BF16)]
    return jnp.concatenate([time_rows(face[:16]), time_rows(face[16:])], axis=0), parts


def write_rows(links, flat_ref, order_ref):
    count = 12 * len(links)
    for index, (_, matrix_re, matrix_im) in enumerate(links):
        flat_ref[index * 96 : index * 96 + 48, :] = matrix_re
        flat_ref[index * 96 + 48 : index * 96 + 96, :] = matrix_im
    long = jnp.concatenate([flat_ref[pl.ds(row, count, stride=8), :] for row in range(8)], axis=1)
    for index, (direction, _, _) in enumerate(links):
        for part in range(2):
            first = (index * 2 + part) * 6
            for third in range(3):
                target = direction * 36 + third * 2 + part
                order_ref[pl.ds(target, 6, stride=6), :] = long[first : first + 6, third * 128 : (third + 1) * 128]


def own_kernel(
    rx_ref, own_ref, start_ref, mix_ref, ga_ref, gauge_ref, turns_ref, spread_ref, rows_ref, left_ref, order_ref, flat_ref
):
    selection = jnp.concatenate(all_rows() + layer_rows(3), axis=0)
    face_links = dot(selection, ga_ref[...]).astype(BF16)
    picked = dot(face_links, link_pick()).astype(BF16)
    link_rows = []
    for axis in range(3):
        first = 128 + 32 * axis
        for part in range(2):
            for step in range(4):
                piece = axis * 4 + step
                link_rows.append(picked[first + 16 * part : first + 16 * part + 16, piece * 128 : piece * 128 + 16])
    link_rows.append(picked[:128, 12 * 128 : 12 * 128 + 16])
    gauge = dot(jnp.concatenate(link_rows, axis=0), link_spread()).astype(BF16)
    gauge_ref[...] = gauge[128:384]
    turns = colour_turns()
    turns_ref[...] = turns
    spread_matrix = mixing_spread()
    spread_ref[...] = spread_matrix
    mix = mix_ref[...]
    zero = jnp.zeros((NVEC, NVEC), F32)
    left = []
    for part in range(2):
        first = mix[:, part * 24 : part * 24 + 24]
        second = mix[:, 48 + part * 24 : 72 + part * 24]
        left += [jnp.concatenate([first, zero], axis=1), jnp.concatenate([zero, second], axis=1)]
    left = jnp.concatenate(bf16_parts(jnp.concatenate(left, axis=0), 2), axis=0)
    left_ref[...] = left
    rows = []
    for axis in range(4):
        mine = own_ref[axis]
        rows.append(jnp.concatenate([mine, mine], axis=0).T)
    rows_ref[0] = rows[1]
    rows_ref[1] = rows[2]
    face, mix_x = next_face(rx_ref)
    ahead = jnp.concatenate([face, start_ref[...]], axis=0)
    turned = dot(ahead, turns)
    mixings = spread_mixing([jnp.concatenate(pair, axis=0) for pair in zip(mix_x, bf16_parts(mix, 2))], spread_matrix)
    links = []
    for index, direction in enumerate((0, 3)):
        here = slice(index * 128, index * 128 + 128)
        to_re, to_im = hop(gauge[direction * 128 : direction * 128 + 128], ahead[here], turned[here], 1.0 - 2.0 * index)
        folded = spin_fold(dot(rows[direction], to_re), dot(rows[direction], to_im), direction)
        links.append((direction, *link_matrix(folded, mixings[index], left)))
    order_ref[...] = jnp.zeros((144, 128), F32)
    write_rows(links, flat_ref, order_ref)


def second_kernel(
    rz_ref, ry_ref, gauge_ref, turns_ref, spread_ref, rows_ref, left_ref, start_ref, code_ref, flat_ref, order_ref
):
    order_ref[...] = start_ref[...]
    left = left_ref[...]
    face_y, mix_y = next_face(ry_ref)
    face_z, mix_z = next_face(rz_ref)
    ahead = jnp.concatenate([face_y, face_z], axis=0)
    turned = dot(ahead, turns_ref[...])
    mixings = spread_mixing([jnp.concatenate(pair, axis=0) for pair in zip(mix_y, mix_z)], spread_ref[...])
    links = []
    for index, direction in enumerate((1, 2)):
        here = slice(index * 128, index * 128 + 128)
        to_re, to_im = hop(gauge_ref[here, :], ahead[here], turned[here], 1.0)
        rows = rows_ref[index]
        folded = spin_fold(dot(rows, to_re), dot(rows, to_im), direction)
        links.append((direction, *link_matrix(folded, mixings[index], left)))
    write_rows(links, flat_ref, order_ref)
    powers = []
    for block in range(9):
        values = order_ref[block * 16 : block * 16 + 16, :]
        largest = jnp.max(jnp.abs(values), axis=0, keepdims=True)
        power = jnp.clip(jnp.ceil(jnp.log2(jnp.maximum(largest, 1e-30)) + 1e-3), -100.0, 120.0)
        scaled = values * jnp.exp2(-power) * 32767.0
        scaled = jnp.clip(jnp.round(scaled), -32767.0, 32767.0)
        code_ref[block * 16 : block * 16 + 16, :] = scaled.astype(jnp.int32).astype(jnp.int16)
        powers.append(power)
    powers = jnp.concatenate(powers + [jnp.zeros((7, 128), F32)], axis=0)
    code_ref[144:160, :] = powers.astype(jnp.int32).astype(jnp.int16)


def place_kernel(order, site_ref, code_ref, out_ref, wide_ref, source_ref, sem_ref):
    for index in range(COUNT):
        source_ref[site_ref[0, order[index]]] = index
    copies = []
    for site in range(COUNT):
        source = source_ref[site]
        power = code_ref[source, 144:160, :].astype(jnp.int32).astype(F32)
        scale = jnp.exp2(power) * (1.0 / 32767.0)
        for block in range(9):
            values = code_ref[source, block * 16 : block * 16 + 16, :].astype(jnp.int32).astype(F32)
            wide_ref[site, block * 16 : block * 16 + 16, :] = values * scale[block : block + 1]
        if site % CHUNK == CHUNK - 1:
            here = pl.ds(site - CHUNK + 1, CHUNK)
            copy = pltpu.make_async_copy(wide_ref.at[here], out_ref.at[here], sem_ref.at[site // CHUNK])
            copy.start()
            copies.append(copy)
    for copy in copies:
        copy.wait()


def first_call(block):
    return pl.pallas_call(
        first_kernel,
        out_shape=[
            jax.ShapeDtypeStruct((4, 128, WIDE), BF16),
            jax.ShapeDtypeStruct((128, WIDE), BF16),
            jax.ShapeDtypeStruct((NVEC, 128), F32),
        ]
        + [jax.ShapeDtypeStruct((SENT, 128), BF16)] * 3,
        compiler_params=pltpu.CompilerParams(vmem_limit_bytes=40 * 2**20),
        name="gram_and_mixing",
    )(block)


def own_call(face_x, own, start, mix, gauge):
    return pl.pallas_call(
        own_kernel,
        out_shape=[
            jax.ShapeDtypeStruct((256, 3 * PAD), BF16),
            jax.ShapeDtypeStruct((WIDE, 2 * PAD), BF16),
            jax.ShapeDtypeStruct((128, 4 * PAD), BF16),
            jax.ShapeDtypeStruct((2, WIDE, 256), BF16),
            jax.ShapeDtypeStruct((192, 48), BF16),
            jax.ShapeDtypeStruct((144, 128), F32),
        ],
        scratch_shapes=[pltpu.VMEM((192, 48), F32)],
        compiler_params=pltpu.CompilerParams(vmem_limit_bytes=40 * 2**20),
        cost_estimate=pl.CostEstimate(flops=2 * 10**9, bytes_accessed=4 * 10**6, transcendentals=0),
        name="own_part",
    )(face_x, own, start, mix, gauge)


def second_call(face_y, face_z, prepared):
    return pl.pallas_call(
        second_kernel,
        out_shape=jax.ShapeDtypeStruct((160, 128), jnp.int16),
        scratch_shapes=[pltpu.VMEM((192, 48), F32), pltpu.VMEM((144, 128), F32)],
        compiler_params=pltpu.CompilerParams(vmem_limit_bytes=40 * 2**20),
        name="coarse_links",
    )(face_z, face_y, *prepared)


def place_call(site_map, codes, order):
    return pl.pallas_call(
        lambda *refs: place_kernel(order, *refs),
        in_specs=[pl.BlockSpec(memory_space=pltpu.SMEM), pl.BlockSpec(memory_space=pltpu.VMEM)],
        out_specs=pl.BlockSpec(memory_space=pl.ANY),
        out_shape=jax.ShapeDtypeStruct((COUNT, 144, 128), F32),
        scratch_shapes=[
            pltpu.VMEM((COUNT, 144, 128), F32),
            pltpu.SMEM((COUNT,), jnp.int32),
            pltpu.SemaphoreType.DMA((COUNT // CHUNK,)),
        ],
        compiler_params=pltpu.CompilerParams(vmem_limit_bytes=40 * 2**20),
        name="place_links",
    )(site_map, codes)


def passed_back(value, axis):
    count = lax.axis_size(axis)
    return lax.ppermute(value, axis, [(source, (source - 1) % count) for source in range(count)])


def flat_index(z, core):
    return (z % 4) * 8 + (z // 4) * 2 + core


def gathered(code):
    pairs = [[flat_index(z, core), flat_index(z + 1, core)] for z in range(0, 16, 2) for core in range(2)]
    rings = [[flat_index(z + odd, core) for z in range(0, 16, 2) for core in range(2)] for odd in range(2)]
    names = ("gx", "gy")
    code = lax.all_gather(code[None], names, axis=0, tiled=True, axis_index_groups=pairs)
    code = lax.all_gather(code, names, axis=0, tiled=True, axis_index_groups=rings)
    return code, [index for pair in pairs for index in pair]


def body(near_null, gauge, site_map):
    own, start, mix, face_y, face_x, face_z = first_call(near_null.reshape(2 * SITES, FULL))
    face_y = passed_back(face_y, "gy")
    face_x = passed_back(face_x, "gx")
    face_z = passed_back(face_z, "zt")
    prepared = own_call(face_x, own, start, mix, gauge.reshape(2 * SITES, LINKS))
    code = second_call(face_y, face_z, prepared)
    codes, order = gathered(code)
    placed = place_call(site_map, codes, order)
    placed = placed.reshape(COUNT, 72, 2, 128).transpose(0, 2, 1, 3)
    return placed.reshape(1, COUNT, 2, 9216)


def solution(mesh):
    return jax.shard_map(
        body,
        mesh=mesh,
        in_specs=(P("gx", "gy", "zt", None, None), P("gx", "gy", "zt", None, None), P("zt", None)),
        out_specs=P("zt", None, None, None),
        check_vma=False,
    )
```
